128 devices in a mesh: aa: 16 (over z, x_lo, core), ba: 8 (over y, x_hi).
Axes of the slice: x: 4 (x_hi: 2, x_lo: 2; x = x_hi * 2 + x_lo), y: 4, z: 4, core: 2. Of those that a mesh axis runs over, the one named last changes fastest.
Arguments:
- tensor: bfloat16 [576, 576, 576], P('aa', 'ba'), may hold values from -20 to 20
- trial_x: float32 [576, 24], replicated, may hold values from -0.25 to 0.25
- trial_y: float32 [576, 24], replicated, may hold values from -0.25 to 0.25
Outputs:
- gram_x: float32 [576, 576], P('aa')
- proj_x: float32 [576, 24], P('aa')
- gram_y: float32 [576, 576], P('ba')
- proj_y: float32 [576, 24], P('ba')
The draws below stay inside these ranges and needn't reach their ends.
All inputs are finite; a program needn't handle non-finite values.
Results may differ from the reference program's by a relative error of at most 0.0003.
Values may be sent and summed in bfloat16 or wider, within the bound.
A program may use at most 192 MiB of HBM per device.

```python
import jax
import jax.numpy as jnp
from jax import lax

CHI = 24
PAIR = 576


def draw_tensor(key, part):
    key = jax.random.fold_in(key, 11)
    subkeys = jax.random.split(key, 9)
    side_y = jnp.clip(jax.random.normal(subkeys[0], (CHI, CHI), jnp.float32), -4.0, 4.0)
    side_x = jnp.clip(jax.random.normal(subkeys[1], (CHI, CHI), jnp.float32), -4.0, 4.0)
    core_x = jnp.clip(jax.random.normal(subkeys[2], (CHI, CHI, CHI), jnp.float32), -4.0, 4.0)
    core_y = jnp.clip(jax.random.normal(subkeys[3], (CHI, CHI, CHI), jnp.float32), -4.0, 4.0)
    weight_u = jax.random.uniform(subkeys[4], (CHI, CHI), jnp.float32, 0.5, 1.5)
    weight_h = jax.random.uniform(subkeys[5], (CHI, CHI), jnp.float32, 0.5, 1.5)
    weight_v = jax.random.uniform(subkeys[6], (CHI, CHI), jnp.float32, 0.5, 1.5)
    weight_g = jax.random.uniform(subkeys[7], (CHI, CHI), jnp.float32, 0.5, 1.5)
    noise_part = 0.5 * jnp.clip(jax.random.normal(subkeys[8], (PAIR, PAIR, PAIR), jnp.float32), -4.0, 4.0)
    first_term = 0.7 * side_y[None, None, :, :, None, None] * core_x[:, None, None, None, :, :] * weight_u[None, :, None, None, :, None] * weight_h[None, :, None, None, None, :]
    second_term = 0.7 * side_x[:, :, None, None, None, None] * core_y[None, None, :, None, :, :] * weight_v[None, None, None, :, :, None] * weight_g[None, None, None, :, None, :]
    structured = (first_term + second_term).reshape(PAIR, PAIR, PAIR)
    return jnp.clip(noise_part + structured, -20.0, 20.0).astype(jnp.bfloat16)


def noise(stream_key, extent, scale, bound, kind=jnp.bfloat16):
    entries = scale * jax.random.normal(stream_key, extent, jnp.float32)
    return jnp.clip(entries, min=-bound, max=bound).astype(kind)


def setup_inputs(seed: int = 0) -> dict:
    key_of = jax.random.split(jax.random.key(seed), 4)
    return {
        "tensor": draw_tensor(jax.random.fold_in(key_of[3], 71), 0),
        "trial_x": noise(key_of[1], (PAIR, CHI), PAIR ** -0.5, 0.25, jnp.float32),
        "trial_y": noise(key_of[2], (PAIR, CHI), PAIR ** -0.5, 0.25, jnp.float32),
    }


def leg_grams(tensor, leg_axis):
    legs_view = tensor.reshape(CHI, CHI, CHI, CHI, CHI, CHI)
    summed_axes = (1, 2) if leg_axis == 0 else (0, 1)

    def accumulate(totals, position):
        layer_slice = lax.dynamic_index_in_dim(legs_view, position, leg_axis + 1, keepdims=False).astype(jnp.float32)
        upper_view = jnp.transpose(layer_slice, (leg_axis, 4) + summed_axes + (3,)).reshape(PAIR, PAIR * CHI)
        lower_view = jnp.transpose(layer_slice, (leg_axis, 3) + summed_axes + (4,)).reshape(PAIR, PAIR * CHI)
        upper_sum = totals[0] + jnp.dot(upper_view, upper_view.T, precision=lax.Precision.HIGHEST, preferred_element_type=jnp.float32)
        lower_sum = totals[1] + jnp.dot(lower_view, lower_view.T, precision=lax.Precision.HIGHEST, preferred_element_type=jnp.float32)
        return (upper_sum, lower_sum), None

    start_zero = jnp.zeros((PAIR, PAIR), jnp.float32)
    totals, _ = lax.scan(accumulate, (start_zero, start_zero), jnp.arange(CHI, dtype=jnp.int32))
    factor = 1.0 / (CHI ** 3)
    return totals[0] * factor, totals[1] * factor


def compose(q_up, q_low):
    up_matrix = q_up.reshape(CHI, CHI, CHI, CHI).transpose(0, 2, 1, 3).reshape(PAIR, PAIR)
    low_matrix = q_low.reshape(CHI, CHI, CHI, CHI).transpose(0, 2, 1, 3).reshape(PAIR, PAIR)
    joined = jnp.dot(up_matrix, low_matrix.T, precision=lax.Precision.HIGHEST, preferred_element_type=jnp.float32)
    return joined.reshape(CHI, CHI, CHI, CHI).transpose(0, 2, 1, 3).reshape(PAIR, PAIR) * (1.0 / (CHI ** 3))


def reference(tensor, trial_x, trial_y):
    qx_up, qx_low = leg_grams(tensor, 0)
    qy_up, qy_low = leg_grams(tensor, 2)
    gram_x = compose(qx_up, qx_low)
    gram_y = compose(qy_up, qy_low)
    proj_x = jnp.dot(gram_x, trial_x, precision=lax.Precision.HIGHEST, preferred_element_type=jnp.float32)
    proj_y = jnp.dot(gram_y, trial_y, precision=lax.Precision.HIGHEST, preferred_element_type=jnp.float32)
    return (gram_x, proj_x, gram_y, proj_y)
```

```python
import functools

import jax
import jax.numpy as jnp
import numpy as np
from jax import lax
from jax.experimental import pallas as pl
from jax.experimental.pallas import tpu as pltpu
from jax.sharding import PartitionSpec as P

CHI = 24
PAIR = 576
GROUPS = 8
MSG = 32
STACK = GROUPS * MSG
HIGHEST = lax.Precision.HIGHEST
MESH = pl.DeviceIdType.MESH
NT = (((1,), (1,)), ((), ()))


def send_rows():
    out = np.zeros((3, STACK, 72), np.float32)
    for jd in range(8):
        for xs in range(3):
            for y in range(3):
                for ys in range(3):
                    out[xs, jd * MSG + xs * 9 + y * 3 + ys, y * 24 + jd * 3 + ys] = 1
    return out


def y_rows():
    out = np.zeros((240, 256), np.float32)
    for xg in range(8):
        for xs in range(3):
            for y in range(3):
                for ys in range(3):
                    out[y * 80 + xg * 9 + xs * 3 + ys, xg * 32 + xs * 9 + y * 3 + ys] = 1
    return out


def bond_swap():
    out = np.zeros((PAIR, PAIR), np.float32)
    for a in range(CHI):
        for b in range(CHI):
            out[b * CHI + a, a * CHI + b] = 1
    return out


def enter(others_count, signal_all):
    barrier = pltpu.get_barrier_semaphore()
    signal_all(barrier)
    pl.semaphore_wait(barrier, others_count)


def place():
    aa = lax.axis_index("aa")
    ba = lax.axis_index("ba")
    return aa // 2, aa % 2, ba


def greet_core_group(i, c, j):
    def signal_all(barrier):
        def one(n, carry):
            di = n // 8
            dj = n % 8
            same = jnp.logical_and(di == i, dj == j)
            core = jnp.where(same, 1 - c, c)
            pl.semaphore_signal(
                barrier, inc=1, device_id=(2 * di + core, dj), device_id_type=MESH
            )
            return carry

        lax.fori_loop(0, 64, one, 0)

    enter(64, signal_all)


def gram_kernel(
    t_ref, ps_ref, py_ref, eye_ref, swap_ref, q_ref,
    snd, got, zbuf, m_up, m_low, send_sem, recv_sem, fsend_sem, frecv_sem,
):
    i, c, j = place()
    greet_core_group(i, c, j)

    def gather_unit(u, carry):
        rows = jnp.zeros((STACK, PAIR), jnp.float32)
        for xs in range(3):
            rows += jnp.dot(ps_ref[xs], t_ref[3 * u + xs], preferred_element_type=jnp.float32)
        snd[u] = rows.astype(jnp.bfloat16).reshape(GROUPS, MSG, PAIR)
        return carry

    lax.fori_loop(0, 12, gather_unit, 0)

    def send_unit(u, idest):
        x = 3 * i + (12 * c + u) // 8

        def one(s, carry):
            jd = (j + s) % 8
            same = jnp.logical_and(idest == i, jd == j)

            @pl.when(jnp.logical_not(same))
            def _():
                pltpu.make_async_remote_copy(
                    src_ref=snd.at[u, jd],
                    dst_ref=got.at[x, j],
                    send_sem=send_sem.at[u],
                    recv_sem=recv_sem.at[x],
                    device_id=(2 * idest + c, jd),
                    device_id_type=MESH,
                ).start()

            @pl.when(same)
            def _():
                got[x, j] = snd[u, jd]

            return carry

        lax.fori_loop(0, 8, one, 0)

    def send_to(s, carry):
        idest = (i + s) % 8
        first = (idest + 4 * c) % 8
        send_unit(first, idest)

        @pl.when(first < 4)
        def _():
            send_unit(first + 8, idest)

        return carry

    lax.fori_loop(0, 8, send_to, 0)

    sibling = (2 * i + (1 - c), j)
    direct_one = (i < 4) == (c == 0)

    def forward(x):
        return pltpu.make_async_remote_copy(
            src_ref=got.at[x],
            dst_ref=got.at[x],
            send_sem=fsend_sem.at[x],
            recv_sem=frecv_sem.at[x],
            device_id=sibling,
            device_id_type=MESH,
        )

    def take_direct(x, own):
        @pl.when(own)
        def _():
            pltpu.make_async_copy(
                got.at[x, pl.ds(0, 7)], got.at[x, pl.ds(0, 7)], recv_sem.at[x]
            ).wait()

        @pl.when(jnp.logical_not(own))
        def _():
            pltpu.make_async_copy(got.at[x], got.at[x], recv_sem.at[x]).wait()

        forward(x).start()

    def receive(s, carry):
        src = (i + 8 - s) % 8
        own = src == i
        take_direct(3 * src + 2 * c, own)

        @pl.when(direct_one)
        def _():
            take_direct(3 * src + 1, own)

        return carry

    lax.fori_loop(0, 8, receive, 0)

    def receive_forwarded(src, carry):
        forward(3 * src + 2 * (1 - c)).wait_recv()
        forward(3 * src + 2 * c).wait_send()

        @pl.when(direct_one)
        def _():
            forward(3 * src + 1).wait_send()

        @pl.when(jnp.logical_not(direct_one))
        def _():
            forward(3 * src + 1).wait_recv()

        return carry

    lax.fori_loop(0, 8, receive_forwarded, 0)

    def drain(u, carry):
        idest = (12 * c + u) % 8

        @pl.when(idest == i)
        def _():
            pltpu.make_async_copy(
                snd.at[u, pl.ds(0, 7)], snd.at[u, pl.ds(0, 7)], send_sem.at[u]
            ).wait()

        @pl.when(idest != i)
        def _():
            pltpu.make_async_copy(snd.at[u], snd.at[u], send_sem.at[u]).wait()

        return carry

    lax.fori_loop(0, 12, drain, 0)

    @pl.when(c == 1)
    def _():
        def per_group(jd, carry):
            for g in range(3):
                block = got[pl.ds(8 * g, 8), jd].reshape(256, PAIR)
                rows = jnp.dot(py_ref[...], block, preferred_element_type=jnp.float32)
                rows = rows.astype(jnp.bfloat16)
                for y in range(3):
                    zbuf[3 * jd + y, pl.ds(80 * g, 80)] = rows[80 * y : 80 * y + 80]
            for y in range(3):
                zbuf[3 * jd + y, pl.ds(240, 16)] = jnp.zeros((16, PAIR), jnp.bfloat16)
            return carry

        lax.fori_loop(0, 8, per_group, 0)

    @pl.when(c == 0)
    def _():
        def per_x(x, carry):
            zbuf[x] = got[x].reshape(STACK, PAIR)
            return carry

        lax.fori_loop(0, 24, per_x, 0)

    def turn(p, carry):
        for perm, m in ((eye_ref, m_up), (swap_ref, m_low)):
            one = lax.dot_general(perm[...], zbuf[2 * p], NT, preferred_element_type=jnp.float32)
            two = lax.dot_general(perm[...], zbuf[2 * p + 1], NT, preferred_element_type=jnp.float32)
            for z in range(24):
                rows = jnp.concatenate([one[24 * z : 24 * z + 24], two[24 * z : 24 * z + 24]], 0)
                m[pl.ds(pl.multiple_of(48 * p, 16), 48), 256 * z : 256 * z + 256] = rows.astype(
                    jnp.bfloat16
                )
        return carry

    lax.fori_loop(0, 12, turn, 0)

    for which, m in enumerate((m_up, m_low)):
        for col, width in ((0, 256), (256, 256), (512, 64)):
            def step(kk, total):
                ks = pl.ds(pl.multiple_of(kk * 1024, 1024), 1024)
                return total + lax.dot_general(
                    m[:, ks], m[col : col + width, ks], NT, preferred_element_type=jnp.float32
                )

            total = lax.fori_loop(0, 6, step, jnp.zeros((PAIR, width), jnp.float32))
            q_ref[pl.ds(24 * which, 24), :, col : col + width] = total.reshape(24, 24, width)


def relayout(block, st_ref, mask_ref):
    mask = mask_ref[...]
    spread = (block[:, None, :] * mask[None, :, :]).reshape(PAIR, PAIR)
    high = spread.astype(jnp.bfloat16)
    rest = spread - high.astype(jnp.float32)
    mid = rest.astype(jnp.bfloat16)
    low = (rest - mid.astype(jnp.float32)).astype(jnp.bfloat16)
    st = st_ref[...]
    tiled = (
        jnp.dot(high, st, preferred_element_type=jnp.float32)
        + jnp.dot(mid, st, preferred_element_type=jnp.float32)
        + jnp.dot(low, st, preferred_element_type=jnp.float32)
    )
    return jnp.sum(tiled.reshape(CHI, CHI, PAIR) * mask[:, None, :], axis=0)


def compose_kernel(
    q_ref, st_ref, mask_ref, ox_ref, oy_ref,
    parts, mine, ups, lows, outs, send_sem, recv_sem, out_sem, up_sem, low_sem, xsend_sem, xrecv_sem,
):
    i, c, j = place()
    chip = 8 * i + j
    greet_core_group(i, c, j)
    scale = 1.0 / CHI**3
    unit = chip - 16 * c
    owner = jnp.logical_and(unit >= 0, unit < 48)

    def send(s, carry):
        n = (chip + s) % 64
        q = n - 16 * c

        @pl.when(jnp.logical_and(q >= 0, q < 48))
        def _():
            @pl.when(n != chip)
            def _():
                pltpu.make_async_remote_copy(
                    src_ref=q_ref.at[q],
                    dst_ref=parts.at[chip],
                    send_sem=send_sem,
                    recv_sem=recv_sem,
                    device_id=(2 * (n // 8) + c, n % 8),
                    device_id_type=MESH,
                ).start()

            @pl.when(n == chip)
            def _():
                parts[chip] = q_ref[q]

        return carry

    lax.fori_loop(0, 64, send, 0)

    block_index = jnp.where(c == 0, i, j)

    @pl.when(owner)
    def _():
        pltpu.make_async_copy(parts.at[pl.ds(0, 63)], parts.at[pl.ds(0, 63)], recv_sem).wait()

        def add(n, total):
            return total + parts[n]

        total = lax.fori_loop(0, 64, add, jnp.zeros((CHI, PAIR), jnp.float32))
        mine[...] = relayout(total * scale, st_ref, mask_ref)

    is_up = jnp.logical_and(owner, unit < 24)
    is_low = jnp.logical_and(owner, unit >= 24)

    @pl.when(is_up)
    def _():
        def one(s, carry):
            other = jnp.where(c == 0, (j + s) % 8, (i + s) % 8)
            di = jnp.where(c == 0, unit // 3, other)
            dj = jnp.where(c == 0, other, unit // 3)
            same = jnp.logical_and(di == i, dj == j)

            @pl.when(jnp.logical_not(same))
            def _():
                pltpu.make_async_remote_copy(
                    src_ref=mine,
                    dst_ref=ups.at[unit % 3],
                    send_sem=out_sem,
                    recv_sem=up_sem,
                    device_id=(2 * di + c, dj),
                    device_id_type=MESH,
                ).start()

            @pl.when(same)
            def _():
                ups[unit % 3] = mine[...]

            return carry

        lax.fori_loop(0, 8, one, 0)

    @pl.when(is_low)
    def _():
        def one(s, carry):
            n = (chip + s) % 64
            pltpu.make_async_remote_copy(
                src_ref=mine,
                dst_ref=lows.at[unit - 24],
                send_sem=out_sem,
                recv_sem=low_sem,
                device_id=(2 * (n // 8) + c, n % 8),
                device_id_type=MESH,
            ).start()
            return carry

        lax.fori_loop(1, 64, one, 0)
        lows[unit - 24] = mine[...]

    own_up = jnp.logical_and(is_up, unit // 3 == block_index)

    def take(ref, count, sem):
        pltpu.make_async_copy(ref.at[pl.ds(0, count)], ref.at[pl.ds(0, count)], sem).wait()

    @pl.when(own_up)
    def _():
        take(ups, 2, up_sem)

    @pl.when(jnp.logical_not(own_up))
    def _():
        take(ups, 3, up_sem)

    @pl.when(is_low)
    def _():
        take(lows, 23, low_sem)

    @pl.when(jnp.logical_not(is_low))
    def _():
        take(lows, 24, low_sem)

    outs[c] = lax.dot_general(
        ups[...].reshape(72, PAIR), lows[...].reshape(PAIR, PAIR), NT,
        precision=HIGHEST, preferred_element_type=jnp.float32,
    ) * scale
    swap = pltpu.make_async_remote_copy(
        src_ref=outs.at[c],
        dst_ref=outs.at[c],
        send_sem=xsend_sem,
        recv_sem=xrecv_sem,
        device_id=(2 * i + (1 - c), j),
        device_id_type=MESH,
    )
    swap.start()

    @pl.when(owner)
    def _():
        take(q_ref, 47, send_sem)

    @pl.when(jnp.logical_not(owner))
    def _():
        take(q_ref, 48, send_sem)

    @pl.when(is_low)
    def _():
        take(parts, 63, out_sem)

    @pl.when(own_up)
    def _():
        take(parts, 7, out_sem)

    @pl.when(jnp.logical_and(is_up, jnp.logical_not(own_up)))
    def _():
        take(parts, 8, out_sem)

    swap.wait()
    ox_ref[...] = outs[0]
    oy_ref[...] = outs[1]


def per_device(tensor, trial_x, trial_y):
    vmem = pl.BlockSpec(memory_space=pltpu.VMEM)
    dma = pltpu.SemaphoreType.DMA
    factors = pl.pallas_call(
        gram_kernel,
        out_shape=jax.ShapeDtypeStruct((48, CHI, PAIR), jnp.float32),
        in_specs=[vmem] * 5,
        out_specs=vmem,
        scratch_shapes=[
            pltpu.VMEM((12, GROUPS, MSG, PAIR), jnp.bfloat16),
            pltpu.VMEM((24, GROUPS, MSG, PAIR), jnp.bfloat16),
            pltpu.VMEM((24, STACK, PAIR), jnp.bfloat16),
            pltpu.VMEM((PAIR, 24 * 256), jnp.bfloat16),
            pltpu.VMEM((PAIR, 24 * 256), jnp.bfloat16),
            dma((12,)),
            dma((24,)),
            dma((24,)),
            dma((24,)),
        ],
        compiler_params=pltpu.CompilerParams(
            collective_id=0, has_side_effects=True, vmem_limit_bytes=60 * 2**20
        ),
        name="redistribute_and_gram",
    )(
        tensor,
        jnp.asarray(send_rows(), jnp.bfloat16),
        jnp.asarray(y_rows(), jnp.bfloat16),
        jnp.asarray(np.eye(PAIR), jnp.bfloat16),
        jnp.asarray(bond_swap(), jnp.bfloat16),
    )
    index = np.arange(PAIR)
    tile = (index[:, None] % CHI == index[None, :] % CHI).astype(np.float32)
    mask = (np.arange(CHI)[:, None] == index[None, :] // CHI).astype(np.float32)
    out_x, out_y = pl.pallas_call(
        compose_kernel,
        out_shape=[jax.ShapeDtypeStruct((72, PAIR), jnp.float32)] * 2,
        in_specs=[vmem] * 3,
        out_specs=[vmem] * 2,
        scratch_shapes=[
            pltpu.VMEM((64, CHI, PAIR), jnp.float32),
            pltpu.VMEM((CHI, PAIR), jnp.float32),
            pltpu.VMEM((3, CHI, PAIR), jnp.float32),
            pltpu.VMEM((24, CHI, PAIR), jnp.float32),
            pltpu.VMEM((2, 72, PAIR), jnp.float32),
            dma, dma, dma, dma, dma, dma, dma,
        ],
        compiler_params=pltpu.CompilerParams(
            collective_id=1, has_side_effects=True, vmem_limit_bytes=60 * 2**20
        ),
        name="reduce_and_compose",
    )(factors, jnp.asarray(tile, jnp.bfloat16), jnp.asarray(mask, jnp.float32))

    def merged(out):
        return out.reshape(3, CHI, CHI, CHI).transpose(0, 2, 1, 3).reshape(72, PAIR)

    core = lax.axis_index("aa") % 2
    gram_x = lax.dynamic_slice_in_dim(merged(out_x), core * 36, 36, 0)
    gram_y = merged(out_y)
    proj_x = jnp.dot(gram_x, trial_x, precision=HIGHEST, preferred_element_type=jnp.float32)
    proj_y = jnp.dot(gram_y, trial_y, precision=HIGHEST, preferred_element_type=jnp.float32)
    return (gram_x, proj_x, gram_y, proj_y)


def solution(mesh):
    in_specs = (P("aa", "ba", None), P(), P())
    out_specs = (P("aa", None), P("aa", None), P("ba", None), P("ba", None))
    return jax.shard_map(
        per_device, mesh=mesh, in_specs=in_specs, out_specs=out_specs, check_vma=False
    )
```

```python
import functools

import jax
import jax.numpy as jnp
import numpy as np
from jax import lax
from jax.experimental import pallas as pl
from jax.experimental.pallas import tpu as pltpu
from jax.sharding import PartitionSpec as P

CHI = 24
PAIR = 576
GROUPS = 8
MSG = 32
STACK = GROUPS * MSG
HIGHEST = lax.Precision.HIGHEST
MESH = pl.DeviceIdType.MESH
NT = (((1,), (1,)), ((), ()))


def greet_all(i, c, j):
    def signal_all(barrier):
        def one(n, carry):
            pl.semaphore_signal(
                barrier, inc=1, device_id=(n // 8, n % 8), device_id_type=MESH
            )
            return carry

        lax.fori_loop(0, 128, one, 0)

    enter(128, signal_all)


def send_rows():
    out = np.zeros((3, STACK, 72), np.float32)
    for jd in range(8):
        for xs in range(3):
            for y in range(3):
                for ys in range(3):
                    out[xs, jd * MSG + xs * 9 + y * 3 + ys, y * 24 + jd * 3 + ys] = 1
    return out


def y_rows():
    out = np.zeros((240, 256), np.float32)
    for xg in range(8):
        for xs in range(3):
            for y in range(3):
                for ys in range(3):
                    out[y * 80 + xg * 9 + xs * 3 + ys, xg * 32 + xs * 9 + y * 3 + ys] = 1
    return out


def bond_swap():
    out = np.zeros((PAIR, PAIR), np.float32)
    for a in range(CHI):
        for b in range(CHI):
            out[b * CHI + a, a * CHI + b] = 1
    return out


def enter(others_count, signal_all):
    barrier = pltpu.get_barrier_semaphore()
    signal_all(barrier)
    pl.semaphore_wait(barrier, others_count)


def place():
    aa = lax.axis_index("aa")
    ba = lax.axis_index("ba")
    return aa // 2, aa % 2, ba


def coordinates():
    aa = lax.axis_index("aa")
    ba = lax.axis_index("ba")
    return aa // 4, (aa // 2) % 2 + 2 * (ba % 2), ba // 2


def chip_at(z, x, y):
    return 2 * z + x % 2, 2 * y + x // 2


def shifted(k):
    z, x, y = coordinates()
    first, second, third = k % 4, (k // 4) % 4, k // 16
    return chip_at((z + first) % 4, (x + second + first) % 4, (y + third + 2 * second + first) % 4)


def greet_core_group(i, c, j):
    def signal_all(barrier):
        def one(n, carry):
            di = n // 8
            dj = n % 8
            same = jnp.logical_and(di == i, dj == j)
            core = jnp.where(same, 1 - c, c)
            pl.semaphore_signal(
                barrier, inc=1, device_id=(2 * di + core, dj), device_id_type=MESH
            )
            return carry

        lax.fori_loop(0, 64, one, 0)

    enter(64, signal_all)


def gram_kernel(
    t_ref, ps_ref, py_ref, eye_ref, swap_ref, q_ref,
    snd, got, zbuf, m_up, m_low, send_sem, recv_sem, fsend_sem, frecv_sem,
):
    i, c, j = place()
    greet_core_group(i, c, j)

    def gather_unit(u, carry):
        rows = jnp.zeros((STACK, PAIR), jnp.float32)
        for xs in range(3):
            rows += jnp.dot(ps_ref[xs], t_ref[3 * u + xs], preferred_element_type=jnp.float32)
        snd[u] = rows.astype(jnp.bfloat16).reshape(GROUPS, MSG, PAIR)
        return carry

    lax.fori_loop(0, 12, gather_unit, 0)

    def send_unit(u, idest, jdest):
        x = 3 * i + (12 * c + u) // 8
        same = jnp.logical_and(idest == i, jdest == j)

        @pl.when(jnp.logical_not(same))
        def _():
            pltpu.make_async_remote_copy(
                src_ref=snd.at[u, jdest],
                dst_ref=got.at[x, j],
                send_sem=send_sem.at[u],
                recv_sem=recv_sem.at[x],
                device_id=(2 * idest + c, jdest),
                device_id_type=MESH,
            ).start()

        @pl.when(same)
        def _():
            got[x, j] = snd[u, jdest]

    def send_to(k, carry):
        idest, jdest = shifted(k)
        first = (idest + 4 * c) % 8
        send_unit(first, idest, jdest)

        @pl.when(first < 4)
        def _():
            send_unit(first + 8, idest, jdest)

        return carry

    lax.fori_loop(0, 64, send_to, 0)

    sibling = (2 * i + (1 - c), j)
    direct_one = (i < 4) == (c == 0)

    def forward(x):
        return pltpu.make_async_remote_copy(
            src_ref=got.at[x],
            dst_ref=got.at[x],
            send_sem=fsend_sem.at[x],
            recv_sem=frecv_sem.at[x],
            device_id=sibling,
            device_id_type=MESH,
        )

    def take_direct(x, own):
        @pl.when(own)
        def _():
            pltpu.make_async_copy(
                got.at[x, pl.ds(0, 7)], got.at[x, pl.ds(0, 7)], recv_sem.at[x]
            ).wait()

        @pl.when(jnp.logical_not(own))
        def _():
            pltpu.make_async_copy(got.at[x], got.at[x], recv_sem.at[x]).wait()

        forward(x).start()

    def receive(s, carry):
        src = (i + 8 - s) % 8
        own = src == i
        take_direct(3 * src + 2 * c, own)

        @pl.when(direct_one)
        def _():
            take_direct(3 * src + 1, own)

        return carry

    lax.fori_loop(0, 8, receive, 0)

    def receive_forwarded(src, carry):
        forward(3 * src + 2 * (1 - c)).wait_recv()
        forward(3 * src + 2 * c).wait_send()

        @pl.when(direct_one)
        def _():
            forward(3 * src + 1).wait_send()

        @pl.when(jnp.logical_not(direct_one))
        def _():
            forward(3 * src + 1).wait_recv()

        return carry

    lax.fori_loop(0, 8, receive_forwarded, 0)

    def drain(u, carry):
        idest = (12 * c + u) % 8

        @pl.when(idest == i)
        def _():
            pltpu.make_async_copy(
                snd.at[u, pl.ds(0, 7)], snd.at[u, pl.ds(0, 7)], send_sem.at[u]
            ).wait()

        @pl.when(idest != i)
        def _():
            pltpu.make_async_copy(snd.at[u], snd.at[u], send_sem.at[u]).wait()

        return carry

    lax.fori_loop(0, 12, drain, 0)

    @pl.when(c == 1)
    def _():
        def per_group(jd, carry):
            for g in range(3):
                block = got[pl.ds(8 * g, 8), jd].reshape(256, PAIR)
                rows = jnp.dot(py_ref[...], block, preferred_element_type=jnp.float32)
                rows = rows.astype(jnp.bfloat16)
                for y in range(3):
                    zbuf[3 * jd + y, pl.ds(80 * g, 80)] = rows[80 * y : 80 * y + 80]
            for y in range(3):
                zbuf[3 * jd + y, pl.ds(240, 16)] = jnp.zeros((16, PAIR), jnp.bfloat16)
            return carry

        lax.fori_loop(0, 8, per_group, 0)

    @pl.when(c == 0)
    def _():
        def per_x(x, carry):
            zbuf[x] = got[x].reshape(STACK, PAIR)
            return carry

        lax.fori_loop(0, 24, per_x, 0)

    def turn(p, carry):
        for perm, m in ((eye_ref, m_up), (swap_ref, m_low)):
            one = lax.dot_general(perm[...], zbuf[2 * p], NT, preferred_element_type=jnp.float32)
            two = lax.dot_general(perm[...], zbuf[2 * p + 1], NT, preferred_element_type=jnp.float32)
            for z in range(24):
                rows = jnp.concatenate([one[24 * z : 24 * z + 24], two[24 * z : 24 * z + 24]], 0)
                m[pl.ds(pl.multiple_of(48 * p, 16), 48), 256 * z : 256 * z + 256] = rows.astype(
                    jnp.bfloat16
                )
        return carry

    lax.fori_loop(0, 12, turn, 0)

    for which, m in enumerate((m_up, m_low)):
        for col, width in ((0, 256), (256, 256), (512, 64)):
            def step(kk, total):
                ks = pl.ds(pl.multiple_of(kk * 1024, 1024), 1024)
                return total + lax.dot_general(
                    m[:, ks], m[col : col + width, ks], NT, preferred_element_type=jnp.float32
                )

            total = lax.fori_loop(0, 6, step, jnp.zeros((PAIR, width), jnp.float32))
            q_ref[pl.ds(24 * which, 24), :, col : col + width] = total.reshape(24, 24, width)


def relayout(block, st_ref, mask_ref):
    mask = mask_ref[...]
    spread = (block[:, None, :] * mask[None, :, :]).reshape(PAIR, PAIR)
    high = spread.astype(jnp.bfloat16)
    rest = spread - high.astype(jnp.float32)
    mid = rest.astype(jnp.bfloat16)
    low = (rest - mid.astype(jnp.float32)).astype(jnp.bfloat16)
    st = st_ref[...]
    tiled = (
        jnp.dot(high, st, preferred_element_type=jnp.float32)
        + jnp.dot(mid, st, preferred_element_type=jnp.float32)
        + jnp.dot(low, st, preferred_element_type=jnp.float32)
    )
    return jnp.sum(tiled.reshape(CHI, CHI, PAIR) * mask[:, None, :], axis=0)


def compose_kernel(
    q_ref, st_ref, mask_ref, ox_ref, oy_ref,
    parts1, parts2, parts3, sums1, sums2, mine, ups, lows, piece,
    s1_sem, r1_sem, s2_sem, r2_sem, s3_sem, r3_sem, out_sem, up_sem, low_sem, x_sem, rx_sem, ry_sem,
):
    i, c, j = place()
    greet_all(i, c, j)
    scale = 1.0 / CHI**3
    here = coordinates()

    def moved(axis, to):
        to_coords = [to if a == axis else here[a] for a in range(3)]
        di, dj = chip_at(*to_coords)
        return 2 * di + c, dj

    def axes(part):
        return part, (part + 1) % 3, (part + 2) % 3

    def others(axis, body):
        def one(s, carry):
            body((here[axis] + s) % 4)
            return carry

        lax.fori_loop(1, 4, one, 0)

    def wait_for(ref, sem):
        pltpu.make_async_copy(ref, ref, sem).wait()

    for part in range(3):
        first = axes(part)[0]

        def send(to, part=part, first=first):
            pltpu.make_async_remote_copy(
                src_ref=q_ref.at[pl.ds(16 * part + 4 * to, 4)],
                dst_ref=parts1.at[part, here[first]],
                send_sem=s1_sem.at[part],
                recv_sem=r1_sem.at[part],
                device_id=moved(first, to),
                device_id_type=MESH,
            ).start()

        others(first, send)
        parts1[part, here[first]] = q_ref[pl.ds(16 * part + 4 * here[first], 4)]

    for part in range(3):
        second = axes(part)[1]
        wait_for(parts1.at[part, pl.ds(0, 3)], r1_sem.at[part])
        sums1[part] = (parts1[part, 0] + parts1[part, 1]) + (parts1[part, 2] + parts1[part, 3])

        def send(to, part=part, second=second):
            pltpu.make_async_remote_copy(
                src_ref=sums1.at[part, to],
                dst_ref=parts2.at[part, here[second]],
                send_sem=s2_sem.at[part],
                recv_sem=r2_sem.at[part],
                device_id=moved(second, to),
                device_id_type=MESH,
            ).start()

        others(second, send)
        parts2[part, here[second]] = sums1[part, here[second]]

    owned = (here[0] + here[1] + here[2]) % 4
    for part in range(3):
        third = axes(part)[2]
        wait_for(parts2.at[part, pl.ds(0, 3)], r2_sem.at[part])
        sums2[part] = (parts2[part, 0] + parts2[part, 1]) + (parts2[part, 2] + parts2[part, 3])

        @pl.when(owned == part)
        def _(part=part, third=third):
            parts3[here[third]] = sums2[part]

        @pl.when(owned != part)
        def _(part=part, third=third):
            to = (part + 8 - here[axes(part)[0]] - here[axes(part)[1]]) % 4
            pltpu.make_async_remote_copy(
                src_ref=sums2.at[part],
                dst_ref=parts3.at[here[third]],
                send_sem=s3_sem.at[part],
                recv_sem=r3_sem,
                device_id=moved(third, to),
                device_id_type=MESH,
            ).start()

    unit = 16 * owned + 4 * jnp.where(
        owned == 0, here[0], jnp.where(owned == 1, here[1], here[2])
    ) + jnp.where(owned == 0, here[1], jnp.where(owned == 1, here[2], here[0]))
    owner = owned < 3

    @pl.when(owner)
    def _():
        wait_for(parts3.at[pl.ds(0, 3)], r3_sem)
        total = (parts3[0] + parts3[1]) + (parts3[2] + parts3[3])
        mine[...] = relayout(total * scale, st_ref, mask_ref)

    is_up = jnp.logical_and(owner, unit < 24)
    is_low = jnp.logical_and(owner, unit >= 24)
    local = jnp.where(is_up, unit, unit - 24)
    by_i = is_up == (c == 0)
    block = local // 3
    keeps = jnp.logical_and(owner, jnp.where(by_i, i, j) == block)

    def deliver(slots, sem):
        def one(s, carry):
            other = jnp.where(by_i, (j + s) % 8, (i + s) % 8)
            di = jnp.where(by_i, block, other)
            dj = jnp.where(by_i, other, block)
            same = jnp.logical_and(di == i, dj == j)

            @pl.when(jnp.logical_not(same))
            def _():
                pltpu.make_async_remote_copy(
                    src_ref=mine,
                    dst_ref=slots.at[local % 3],
                    send_sem=out_sem,
                    recv_sem=sem,
                    device_id=(2 * di + c, dj),
                    device_id_type=MESH,
                ).start()

            @pl.when(same)
            def _():
                slots[local % 3] = mine[...]

            return carry

        lax.fori_loop(0, 8, one, 0)

    @pl.when(is_up)
    def _():
        deliver(ups, up_sem)

    @pl.when(is_low)
    def _():
        deliver(lows, low_sem)

    def take(ref, count, sem):
        wait_for(ref.at[pl.ds(0, count)], sem)

    def take_rows(slots, kept, sem):
        @pl.when(kept)
        def _():
            take(slots, 2, sem)

        @pl.when(jnp.logical_not(kept))
        def _():
            take(slots, 3, sem)

    take_rows(ups, jnp.logical_and(keeps, is_up), up_sem)
    take_rows(lows, jnp.logical_and(keeps, is_low), low_sem)

    piece[...] = lax.dot_general(
        ups[...].reshape(72, PAIR), lows[...].reshape(72, PAIR), NT,
        precision=HIGHEST, preferred_element_type=jnp.float32,
    ) * scale

    def spread(out_ref, slot, sem):
        def one(s, carry):
            core = (c + s) % 2
            other = s // 2
            di = jnp.where(c == 0, i, (i + other) % 8)
            dj = jnp.where(c == 0, (j + other) % 8, j)
            pltpu.make_async_remote_copy(
                src_ref=piece,
                dst_ref=out_ref.at[slot],
                send_sem=x_sem.at[s % 2],
                recv_sem=sem,
                device_id=(2 * di + core, dj),
                device_id_type=MESH,
            ).start()
            return carry

        lax.fori_loop(1, 16, one, 0)
        out_ref[slot] = piece[...]

    @pl.when(c == 0)
    def _():
        spread(ox_ref, j, rx_sem)

    @pl.when(c == 1)
    def _():
        spread(oy_ref, i, ry_sem)

    for part in range(3):
        wait_for(q_ref.at[pl.ds(0, 12)], s1_sem.at[part])
        wait_for(sums1.at[part, pl.ds(0, 3)], s2_sem.at[part])

        @pl.when(owned != part)
        def _(part=part):
            wait_for(sums2.at[part], s3_sem.at[part])

    @pl.when(keeps)
    def _():
        take(q_ref, 7, out_sem)

    @pl.when(jnp.logical_and(owner, jnp.logical_not(keeps)))
    def _():
        take(q_ref, 8, out_sem)

    take(ox_ref, 7, x_sem.at[0])
    take(ox_ref, 8, x_sem.at[1])

    @pl.when(c == 0)
    def _():
        take(ox_ref, 7, rx_sem)
        take(oy_ref, 8, ry_sem)

    @pl.when(c == 1)
    def _():
        take(ox_ref, 8, rx_sem)
        take(oy_ref, 7, ry_sem)


def per_device(tensor, trial_x, trial_y):
    vmem = pl.BlockSpec(memory_space=pltpu.VMEM)
    dma = pltpu.SemaphoreType.DMA
    factors = pl.pallas_call(
        gram_kernel,
        out_shape=jax.ShapeDtypeStruct((48, CHI, PAIR), jnp.float32),
        in_specs=[vmem] * 5,
        out_specs=vmem,
        scratch_shapes=[
            pltpu.VMEM((12, GROUPS, MSG, PAIR), jnp.bfloat16),
            pltpu.VMEM((24, GROUPS, MSG, PAIR), jnp.bfloat16),
            pltpu.VMEM((24, STACK, PAIR), jnp.bfloat16),
            pltpu.VMEM((PAIR, 24 * 256), jnp.bfloat16),
            pltpu.VMEM((PAIR, 24 * 256), jnp.bfloat16),
            dma((12,)),
            dma((24,)),
            dma((24,)),
            dma((24,)),
        ],
        compiler_params=pltpu.CompilerParams(
            collective_id=0, has_side_effects=True, vmem_limit_bytes=60 * 2**20
        ),
        name="redistribute_and_gram",
    )(
        tensor,
        jnp.asarray(send_rows(), jnp.bfloat16),
        jnp.asarray(y_rows(), jnp.bfloat16),
        jnp.asarray(np.eye(PAIR), jnp.bfloat16),
        jnp.asarray(bond_swap(), jnp.bfloat16),
    )
    index = np.arange(PAIR)
    tile = (index[:, None] % CHI == index[None, :] % CHI).astype(np.float32)
    mask = (np.arange(CHI)[:, None] == index[None, :] // CHI).astype(np.float32)
    out_x, out_y = pl.pallas_call(
        compose_kernel,
        out_shape=[jax.ShapeDtypeStruct((8, 72, 72), jnp.float32)] * 2,
        in_specs=[vmem] * 3,
        out_specs=[vmem] * 2,
        scratch_shapes=[
            pltpu.VMEM((3, 4, 4, CHI, PAIR), jnp.float32),
            pltpu.VMEM((3, 4, CHI, PAIR), jnp.float32),
            pltpu.VMEM((4, CHI, PAIR), jnp.float32),
            pltpu.VMEM((3, 4, CHI, PAIR), jnp.float32),
            pltpu.VMEM((3, CHI, PAIR), jnp.float32),
            pltpu.VMEM((CHI, PAIR), jnp.float32),
            pltpu.VMEM((3, CHI, PAIR), jnp.float32),
            pltpu.VMEM((3, CHI, PAIR), jnp.float32),
            pltpu.VMEM((72, 72), jnp.float32),
            dma((3,)), dma((3,)), dma((3,)), dma((3,)), dma((3,)),
            dma, dma, dma, dma, dma((2,)), dma, dma,
        ],
        compiler_params=pltpu.CompilerParams(
            collective_id=1, has_side_effects=True, vmem_limit_bytes=60 * 2**20
        ),
        name="reduce_and_compose",
    )(factors, jnp.asarray(tile, jnp.bfloat16), jnp.asarray(mask, jnp.float32))

    def merged(out):
        return out.reshape(8, 3, CHI, 3, CHI).transpose(1, 0, 3, 2, 4).reshape(72, PAIR)

    core = lax.axis_index("aa") % 2
    gram_x = lax.dynamic_slice_in_dim(merged(out_x), core * 36, 36, 0)
    gram_y = merged(out_y)
    proj_x = jnp.dot(gram_x, trial_x, precision=HIGHEST, preferred_element_type=jnp.float32)
    proj_y = jnp.dot(gram_y, trial_y, precision=HIGHEST, preferred_element_type=jnp.float32)
    return (gram_x, proj_x, gram_y, proj_y)


def solution(mesh):
    in_specs = (P("aa", "ba", None), P(), P())
    out_specs = (P("aa", None), P("aa", None), P("ba", None), P("ba", None))
    return jax.shard_map(
        per_device, mesh=mesh, in_specs=in_specs, out_specs=out_specs, check_vma=False
    )
```

```python
import functools

import jax
import jax.numpy as jnp
import numpy as np
from jax import lax
from jax.experimental import pallas as pl
from jax.experimental.pallas import tpu as pltpu
from jax.sharding import PartitionSpec as P

CHI = 24
PAIR = 576
GROUPS = 8
MSG = 32
STACK = GROUPS * MSG
HIGHEST = lax.Precision.HIGHEST
MESH = pl.DeviceIdType.MESH
NT = (((1,), (1,)), ((), ()))


def send_rows():
    out = np.zeros((STACK, 216), np.float32)
    for jd in range(8):
        for xs in range(3):
            for y in range(3):
                for ys in range(3):
                    h, r = divmod(xs * 9 + y * 3 + ys, 16)
                    out[h * 128 + jd * 16 + r, xs * 72 + y * 24 + jd * 3 + ys] = 1
    return out


def y_rows():
    out = np.zeros((240, 256), np.float32)
    for xg in range(8):
        for xs in range(3):
            for y in range(3):
                for ys in range(3):
                    h, r = divmod(xs * 9 + y * 3 + ys, 16)
                    out[y * 80 + xg * 9 + xs * 3 + ys, h * 128 + xg * 16 + r] = 1
    return out


def place():
    aa = lax.axis_index("aa")
    ba = lax.axis_index("ba")
    return aa // 2, aa % 2, ba


def coordinates():
    aa = lax.axis_index("aa")
    ba = lax.axis_index("ba")
    return aa // 4, (aa // 2) % 2 + 2 * (ba % 2), ba // 2


def chip_at(z, x, y):
    return 2 * z + x % 2, 2 * y + x // 2


def shift_of(k):
    quarter, rest = k // 16, k % 16
    low, high = rest % 4, rest // 4
    dz = 2 * (low % 2) + quarter // 2
    dx = (low + high) % 4
    dy = 2 * ((high + low // 2) % 2) + quarter % 2
    return dz, dx, dy


def partner(k, sign):
    z, x, y = coordinates()
    dz, dx, dy = shift_of(k)
    return chip_at((z + 4 + sign * dz) % 4, (x + 4 + sign * dx) % 4, (y + 4 + sign * dy) % 4)


def wait_for(ref, sem):
    pltpu.make_async_copy(ref, ref, sem).wait()


def take(ref, count, sem):
    wait_for(ref.at[pl.ds(0, count)], sem)


def greet(i, c, j, barrier):
    def one(n, carry):
        di, dj = n // 8, n % 8

        @pl.when(jnp.logical_not(jnp.logical_and(di == i, dj == j)))
        def _():
            pl.semaphore_signal(barrier, inc=1, device_id=(2 * di + c, dj), device_id_type=MESH)

        return carry

    lax.fori_loop(0, 64, one, 0)

    def across(n, carry):
        di = jnp.where(c == 0, n, i)
        dj = jnp.where(c == 0, j, n)
        pl.semaphore_signal(barrier, inc=1, device_id=(2 * di + 1 - c, dj), device_id_type=MESH)
        return carry

    lax.fori_loop(0, 8, across, 0)


def relayout(block, st_ref, mask_ref):
    mask = mask_ref[...]
    spread = (block[:, None, :] * mask[None, :, :]).reshape(PAIR, PAIR)
    high = spread.astype(jnp.bfloat16)
    rest = spread - high.astype(jnp.float32)
    mid = rest.astype(jnp.bfloat16)
    low = (rest - mid.astype(jnp.float32)).astype(jnp.bfloat16)
    st = st_ref[...]
    tiled = (
        jnp.dot(high, st, preferred_element_type=jnp.float32)
        + jnp.dot(mid, st, preferred_element_type=jnp.float32)
        + jnp.dot(low, st, preferred_element_type=jnp.float32)
    )
    return jnp.sum(tiled.reshape(CHI, CHI, PAIR) * mask[:, None, :], axis=0)


def fused_kernel(
    t_ref, ps_ref, py_ref, eye_ref, st_ref, mask_ref, ox_ref, oy_ref,
    snd, got, zbuf, turned, m_up, m_low, q_ref,
    send_sem, recv_sem, fsend_sem, frecv_sem,
    parts1, parts2, parts3, sums1, sums2, mine, ups, lows, piece,
    s1_sem, r1_sem, s2_sem, r2_sem, s3_sem, r3_sem, out_sem, up_sem, low_sem, x_sem, rx_sem, ry_sem,
):
    i, c, j = place()
    here = coordinates()
    barrier = pltpu.get_barrier_semaphore()
    greet(i, c, j, barrier)

    def gather_unit(u, carry):
        rows = jnp.dot(ps_ref[...], t_ref[u], preferred_element_type=jnp.float32)
        rows = rows.astype(jnp.bfloat16)
        for h in range(2):
            for k in range(4):
                snd[u, :, 4 * h + k] = rows[
                    128 * h : 128 * h + 128, 128 * k : 128 * k + 128
                ].reshape(8, 16, 128)
        last = jnp.concatenate([rows[:128, 512:], rows[128:, 512:]], axis=1)
        snd[u, :, 8] = last.reshape(8, 16, 128)
        return carry

    lax.fori_loop(0, 12, gather_unit, 0)
    pl.semaphore_wait(barrier, 71)

    def send_unit(u, k, idest, jdest):
        x = 3 * i + (12 * c + u) // 8

        @pl.when(k > 0)
        def _():
            pltpu.make_async_remote_copy(
                src_ref=snd.at[u, jdest],
                dst_ref=got.at[x, j],
                send_sem=send_sem.at[u],
                recv_sem=recv_sem.at[k],
                device_id=(2 * idest + c, jdest),
                device_id_type=MESH,
            ).start()

        @pl.when(k == 0)
        def _():
            got[x, j] = snd[u, jdest]

    def send_to(k, carry):
        idest, jdest = partner(k, 1)
        first = (idest + 4 * c) % 8
        send_unit(first, k, idest, jdest)

        @pl.when(first < 4)
        def _():
            send_unit(first + 8, k, idest, jdest)

        return carry

    lax.fori_loop(0, 64, send_to, 0)

    two = (i < 4) == (c == 0)
    sibling = (2 * i + (1 - c), j)

    def forward(k, count, core):
        isrc, jsrc = partner(k, -1)
        x = 3 * isrc + jnp.where(core == 0, 0, 3 - count)
        ref = got.at[pl.ds(x, count), jsrc]
        return ref, pltpu.make_async_remote_copy(
            src_ref=ref,
            dst_ref=ref,
            send_sem=fsend_sem.at[k],
            recv_sem=frecv_sem.at[k],
            device_id=sibling,
            device_id_type=MESH,
        )

    def pass_on(k, carry):
        def one(count):
            ref, copy = forward(k, count, c)

            @pl.when(k > 0)
            def _():
                wait_for(ref, recv_sem.at[k])

            copy.start()

        pl.when(two)(lambda: one(2))
        pl.when(jnp.logical_not(two))(lambda: one(1))
        return carry

    def accept(k, carry):
        def one(count):
            forward(k, count, 1 - c)[1].wait_recv()

        pl.when(two)(lambda: one(1))
        pl.when(jnp.logical_not(two))(lambda: one(2))
        return carry

    def finish_forward(k, carry):
        def one(count):
            forward(k, count, c)[1].wait_send()

        pl.when(two)(lambda: one(2))
        pl.when(jnp.logical_not(two))(lambda: one(1))
        return carry

    def stack_x(x):
        for h in range(2):
            for k in range(4):
                zbuf[x, 128 * h : 128 * h + 128, 128 * k : 128 * k + 128] = got[
                    x, :, 4 * h + k
                ].reshape(128, 128)
        last = got[x, :, 8].reshape(128, 128)
        zbuf[x, 0:128, 512:576] = last[:, :64]
        zbuf[x, 128:256, 512:576] = last[:, 64:]

    def stack_y(jd):
        for g in range(3):
            xs = pl.ds(8 * g, 8)
            block = jnp.concatenate(
                [
                    jnp.concatenate(
                        [got[xs, jd, 4 * h + k].reshape(128, 128) for k in range(4)], axis=1
                    )
                    for h in range(2)
                ],
                axis=0,
            )
            rows = jnp.dot(py_ref[...], block, preferred_element_type=jnp.float32)
            last = got[xs, jd, 8].reshape(128, 128)
            tail = (
                jnp.dot(py_ref[:, :128], last, preferred_element_type=jnp.float32)[:, :64]
                + jnp.dot(py_ref[:, 128:], last, preferred_element_type=jnp.float32)[:, 64:]
            )
            rows = jnp.concatenate([rows, tail], axis=1).astype(jnp.bfloat16)
            for y in range(3):
                zbuf[3 * jd + y, 80 * g : 80 * g + 80] = rows[80 * y : 80 * y + 80]
        for y in range(3):
            zbuf[3 * jd + y, 240:256] = jnp.zeros((16, PAIR), jnp.bfloat16)

    def turn(p):
        for w in range(2):
            for start, width in ((0, 256), (256, 256), (512, 64)):
                flat = lax.dot_general(
                    eye_ref[:width, :width],
                    zbuf[2 * p + w, :, start : start + width],
                    NT,
                    preferred_element_type=jnp.float32,
                )
                turned[2 * w, start : start + width] = flat[:, :128]
                turned[2 * w + 1, start : start + width] = flat[:, 128:]
        rows_at = pl.ds(pl.multiple_of(48 * p, 16), 48)
        for z in range(24):
            for half in range(2):
                cols = slice(256 * z + 128 * half, 256 * z + 128 * half + 128)
                straight = [turned[2 * w + half, 24 * z : 24 * z + 24] for w in range(2)]
                m_up[rows_at, cols] = jnp.concatenate(straight, 0).astype(jnp.bfloat16)
                strided = [turned[2 * w + half, pl.ds(z, 24, stride=24)] for w in range(2)]
                m_low[rows_at, cols] = jnp.concatenate(strided, 0).astype(jnp.bfloat16)

    def prepare(core, parity):
        at = here[0] if core == 0 else here[2]

        def per_place(n, carry):
            place_at = (at + parity + 2 * n) % 4

            def per_leg(m, carry):
                stack_x(6 * place_at + m)
                return carry

            def per_block(m, carry):
                stack_y(2 * place_at + m)
                return carry

            if core == 0:
                lax.fori_loop(0, 6, per_leg, 0)
            else:
                lax.fori_loop(0, 2, per_block, 0)

            def per_pair(m, carry):
                turn(3 * place_at + m)
                return carry

            lax.fori_loop(0, 3, per_pair, 0)
            return carry

        lax.fori_loop(0, 2, per_place, 0)

    lax.fori_loop(0, 32, pass_on, 0)
    lax.fori_loop(0, 32, accept, 0)
    pl.when(c == 0)(lambda: prepare(0, 0))
    lax.fori_loop(32, 48, pass_on, 0)
    lax.fori_loop(32, 48, accept, 0)
    pl.when(c == 1)(lambda: prepare(1, 0))
    lax.fori_loop(48, 64, pass_on, 0)
    lax.fori_loop(48, 64, accept, 0)
    pl.when(c == 0)(lambda: prepare(0, 1))
    pl.when(c == 1)(lambda: prepare(1, 1))

    def gram_panel(m, col, width):
        def step(kk, total):
            ks = pl.ds(pl.multiple_of(kk * 2048, 2048), 2048)
            return total + lax.dot_general(
                m[col:, ks], m[col : col + width, ks], NT, preferred_element_type=jnp.float32
            )

        return lax.fori_loop(0, 3, step, jnp.zeros((PAIR - col, width), jnp.float32))

    def gram(which, m):
        base = PAIR * which
        for col, width in ((0, 256), (256, 256), (512, 64)):
            q_ref[base + col : base + PAIR, col : col + width] = gram_panel(m, col, width)
            if col + width < PAIR:
                below = q_ref[base + col + width : base + PAIR, col : col + width]
                q_ref[base + col : base + col + width, col + width :] = below.T

    scale = 1.0 / CHI**3

    def moved(axis, to):
        to_coords = [to if a == axis else here[a] for a in range(3)]
        di, dj = chip_at(*to_coords)
        return 2 * di + c, dj

    def axes(part):
        return part, (part + 1) % 3, (part + 2) % 3

    def others(axis, body):
        def one(s, carry):
            body((here[axis] + s) % 4)
            return carry

        lax.fori_loop(1, 4, one, 0)

    def four(part, to):
        return pl.ds(pl.multiple_of(24 * (16 * part + 4 * to), 8), 96)

    def stage1(part):
        first = axes(part)[0]

        def send(to):
            pltpu.make_async_remote_copy(
                src_ref=q_ref.at[four(part, to)],
                dst_ref=parts1.at[part, here[first]],
                send_sem=s1_sem.at[part],
                recv_sem=r1_sem.at[part],
                device_id=moved(first, to),
                device_id_type=MESH,
            ).start()

        others(first, send)
        parts1[part, here[first]] = q_ref[four(part, here[first])]

    gram(0, m_up)
    stage1(0)
    gram(1, m_low)
    stage1(1)
    stage1(2)

    for part in range(3):
        second = axes(part)[1]
        take(parts1.at[part], 3, r1_sem.at[part])
        total = (parts1[part, 0] + parts1[part, 1]) + (parts1[part, 2] + parts1[part, 3])
        sums1[part] = total.reshape(4, CHI, PAIR)

        def send(to, part=part, second=second):
            pltpu.make_async_remote_copy(
                src_ref=sums1.at[part, to],
                dst_ref=parts2.at[part, here[second]],
                send_sem=s2_sem.at[part],
                recv_sem=r2_sem.at[part],
                device_id=moved(second, to),
                device_id_type=MESH,
            ).start()

        others(second, send)
        parts2[part, here[second]] = sums1[part, here[second]]

    owned = (here[0] + here[1] + here[2]) % 4
    for part in range(3):
        third = axes(part)[2]
        take(parts2.at[part], 3, r2_sem.at[part])
        sums2[part] = (parts2[part, 0] + parts2[part, 1]) + (parts2[part, 2] + parts2[part, 3])

        @pl.when(owned == part)
        def _(part=part, third=third):
            parts3[here[third]] = sums2[part]

        @pl.when(owned != part)
        def _(part=part, third=third):
            to = (part + 8 - here[axes(part)[0]] - here[axes(part)[1]]) % 4
            pltpu.make_async_remote_copy(
                src_ref=sums2.at[part],
                dst_ref=parts3.at[here[third]],
                send_sem=s3_sem.at[part],
                recv_sem=r3_sem,
                device_id=moved(third, to),
                device_id_type=MESH,
            ).start()

    unit = 16 * owned + 4 * jnp.where(
        owned == 0, here[0], jnp.where(owned == 1, here[1], here[2])
    ) + jnp.where(owned == 0, here[1], jnp.where(owned == 1, here[2], here[0]))
    owner = owned < 3

    @pl.when(owner)
    def _():
        wait_for(parts3.at[pl.ds(0, 3)], r3_sem)
        total = (parts3[0] + parts3[1]) + (parts3[2] + parts3[3])
        mine[...] = relayout(total * scale, st_ref, mask_ref)

    is_up = jnp.logical_and(owner, unit < 24)
    is_low = jnp.logical_and(owner, unit >= 24)
    local = jnp.where(is_up, unit, unit - 24)
    by_i = is_up == (c == 0)
    block = local // 3
    keeps = jnp.logical_and(owner, jnp.where(by_i, i, j) == block)

    def deliver(slots, sem):
        def one(s, carry):
            other = jnp.where(by_i, (j + s) % 8, (i + s) % 8)
            di = jnp.where(by_i, block, other)
            dj = jnp.where(by_i, other, block)
            same = jnp.logical_and(di == i, dj == j)

            @pl.when(jnp.logical_not(same))
            def _():
                pltpu.make_async_remote_copy(
                    src_ref=mine,
                    dst_ref=slots.at[local % 3],
                    send_sem=out_sem,
                    recv_sem=sem,
                    device_id=(2 * di + c, dj),
                    device_id_type=MESH,
                ).start()

            @pl.when(same)
            def _():
                slots[local % 3] = mine[...]

            return carry

        lax.fori_loop(0, 8, one, 0)

    @pl.when(is_up)
    def _():
        deliver(ups, up_sem)

    @pl.when(is_low)
    def _():
        deliver(lows, low_sem)

    def take_rows(slots, kept, sem):
        @pl.when(kept)
        def _():
            take(slots, 2, sem)

        @pl.when(jnp.logical_not(kept))
        def _():
            take(slots, 3, sem)

    take_rows(ups, jnp.logical_and(keeps, is_up), up_sem)
    take_rows(lows, jnp.logical_and(keeps, is_low), low_sem)

    piece[...] = lax.dot_general(
        ups[...].reshape(72, PAIR), lows[...].reshape(72, PAIR), NT,
        precision=HIGHEST, preferred_element_type=jnp.float32,
    ) * scale

    def spread(out_ref, slot, sem):
        def one(s, carry):
            core = (c + s) % 2
            other = s // 2
            di = jnp.where(c == 0, i, (i + other) % 8)
            dj = jnp.where(c == 0, (j + other) % 8, j)
            pltpu.make_async_remote_copy(
                src_ref=piece,
                dst_ref=out_ref.at[slot],
                send_sem=x_sem.at[s % 2],
                recv_sem=sem,
                device_id=(2 * di + core, dj),
                device_id_type=MESH,
            ).start()
            return carry

        lax.fori_loop(1, 16, one, 0)
        out_ref[slot] = piece[...]

    @pl.when(c == 0)
    def _():
        spread(ox_ref, j, rx_sem)

    @pl.when(c == 1)
    def _():
        spread(oy_ref, i, ry_sem)

    for part in range(3):
        take(parts1.at[part], 3, s1_sem.at[part])
        wait_for(sums1.at[part, pl.ds(0, 3)], s2_sem.at[part])

        @pl.when(owned != part)
        def _(part=part):
            wait_for(sums2.at[part], s3_sem.at[part])

    @pl.when(keeps)
    def _():
        wait_for(q_ref.at[pl.ds(0, 7 * CHI)], out_sem)

    @pl.when(jnp.logical_and(owner, jnp.logical_not(keeps)))
    def _():
        wait_for(q_ref.at[pl.ds(0, 8 * CHI)], out_sem)

    lax.fori_loop(0, 64, finish_forward, 0)

    def drain(u, carry):
        idest = (12 * c + u) % 8
        pl.when(idest == i)(lambda: take(snd.at[u], 7, send_sem.at[u]))
        pl.when(idest != i)(lambda: take(snd.at[u], 8, send_sem.at[u]))
        return carry

    lax.fori_loop(0, 12, drain, 0)

    take(ox_ref, 7, x_sem.at[0])
    take(ox_ref, 8, x_sem.at[1])

    @pl.when(c == 0)
    def _():
        take(ox_ref, 7, rx_sem)
        take(oy_ref, 8, ry_sem)

    @pl.when(c == 1)
    def _():
        take(ox_ref, 8, rx_sem)
        take(oy_ref, 7, ry_sem)


def per_device(tensor, trial_x, trial_y):
    vmem = pl.BlockSpec(memory_space=pltpu.VMEM)
    dma = pltpu.SemaphoreType.DMA
    index = np.arange(PAIR)
    tile = (index[:, None] % CHI == index[None, :] % CHI).astype(np.float32)
    mask = (np.arange(CHI)[:, None] == index[None, :] // CHI).astype(np.float32)
    f32, bf16 = jnp.float32, jnp.bfloat16
    out_x, out_y = pl.pallas_call(
        fused_kernel,
        out_shape=[jax.ShapeDtypeStruct((8, 72, 72), f32)] * 2,
        in_specs=[vmem] * 6,
        out_specs=[vmem] * 2,
        scratch_shapes=[
            pltpu.VMEM((12, 8, 9, 16, 128), bf16),
            pltpu.VMEM((24, 8, 9, 16, 128), bf16),
            pltpu.VMEM((24, STACK, PAIR), bf16),
            pltpu.VMEM((4, PAIR, 128), f32),
            pltpu.VMEM((PAIR, 24 * 256), bf16),
            pltpu.VMEM((PAIR, 24 * 256), bf16),
            pltpu.VMEM((2 * PAIR, PAIR), f32),
            dma((12,)), dma((64,)), dma((64,)), dma((64,)),
            pltpu.VMEM((3, 4, 4 * CHI, PAIR), f32),
            pltpu.VMEM((3, 4, CHI, PAIR), f32),
            pltpu.VMEM((4, CHI, PAIR), f32),
            pltpu.VMEM((3, 4, CHI, PAIR), f32),
            pltpu.VMEM((3, CHI, PAIR), f32),
            pltpu.VMEM((CHI, PAIR), f32),
            pltpu.VMEM((3, CHI, PAIR), f32),
            pltpu.VMEM((3, CHI, PAIR), f32),
            pltpu.VMEM((72, 72), f32),
            dma((3,)), dma((3,)), dma((3,)), dma((3,)), dma((3,)),
            dma, dma, dma, dma, dma((2,)), dma, dma,
        ],
        compiler_params=pltpu.CompilerParams(
            collective_id=0, has_side_effects=True, vmem_limit_bytes=62 * 2**20
        ),
        name="hotrg_step",
    )(
        tensor.reshape(12, 216, PAIR),
        jnp.asarray(send_rows(), bf16),
        jnp.asarray(y_rows(), bf16),
        jnp.asarray(np.eye(256), bf16),
        jnp.asarray(tile, bf16),
        jnp.asarray(mask, f32),
    )

    def merged(out):
        return out.reshape(8, 3, CHI, 3, CHI).transpose(1, 0, 3, 2, 4).reshape(72, PAIR)

    core = lax.axis_index("aa") % 2
    gram_x = lax.dynamic_slice_in_dim(merged(out_x), core * 36, 36, 0)
    gram_y = merged(out_y)
    proj_x = jnp.dot(gram_x, trial_x, precision=HIGHEST, preferred_element_type=jnp.float32)
    proj_y = jnp.dot(gram_y, trial_y, precision=HIGHEST, preferred_element_type=jnp.float32)
    return (gram_x, proj_x, gram_y, proj_y)


def solution(mesh):
    in_specs = (P("aa", "ba", None), P(), P())
    out_specs = (P("aa", None), P("aa", None), P("ba", None), P("ba", None))
    return jax.shard_map(
        per_device, mesh=mesh, in_specs=in_specs, out_specs=out_specs, check_vma=False
    )
```

```python
import functools

import jax
import jax.numpy as jnp
import numpy as np
from jax import lax
from jax.experimental import pallas as pl
from jax.experimental.pallas import tpu as pltpu
from jax.sharding import PartitionSpec as P

CHI = 24
PAIR = 576
GROUPS = 8
MSG = 32
STACK = GROUPS * MSG
HIGHEST = lax.Precision.HIGHEST
MESH = pl.DeviceIdType.MESH
NT = (((1,), (1,)), ((), ()))


def send_rows():
    out = np.zeros((STACK, 216), np.float32)
    for jd in range(8):
        for xs in range(3):
            for y in range(3):
                for ys in range(3):
                    h, r = divmod(xs * 9 + y * 3 + ys, 16)
                    out[h * 128 + jd * 16 + r, xs * 72 + y * 24 + jd * 3 + ys] = 1
    return out


def y_rows():
    out = np.zeros((192, 192), np.float32)
    for xg in range(6):
        for xs in range(3):
            for y in range(3):
                for ys in range(3):
                    h, r = divmod(xs * 9 + y * 3 + ys, 16)
                    out[y * 64 + xg * 9 + xs * 3 + ys, h * 96 + xg * 16 + r] = 1
    return out


def place():
    aa = lax.axis_index("aa")
    ba = lax.axis_index("ba")
    return aa // 2, aa % 2, ba


def coordinates():
    aa = lax.axis_index("aa")
    ba = lax.axis_index("ba")
    return aa // 4, (aa // 2) % 2 + 2 * (ba % 2), ba // 2


def chip_at(z, x, y):
    return 2 * z + x % 2, 2 * y + x // 2


def shift_of(k):
    quarter, rest = k // 16, k % 16
    low, high = rest % 4, rest // 4
    dz = 2 * (low % 2) + quarter // 2
    dx = (low + high) % 4
    dy = 2 * ((high + low // 2) % 2) + quarter % 2
    return dz, dx, dy


def partner(k, sign):
    z, x, y = coordinates()
    dz, dx, dy = shift_of(k)
    return chip_at((z + 4 + sign * dz) % 4, (x + 4 + sign * dx) % 4, (y + 4 + sign * dy) % 4)


def wait_for(ref, sem):
    pltpu.make_async_copy(ref, ref, sem).wait()


def take(ref, count, sem):
    wait_for(ref.at[pl.ds(0, count)], sem)


def greet(i, c, j, barrier):
    def one(n, carry):
        di, dj = n // 8, n % 8

        @pl.when(jnp.logical_not(jnp.logical_and(di == i, dj == j)))
        def _():
            pl.semaphore_signal(barrier, inc=1, device_id=(2 * di + c, dj), device_id_type=MESH)

        return carry

    lax.fori_loop(0, 64, one, 0)

    @pl.when(c == 0)
    def _():
        pl.semaphore_signal(barrier, inc=1, device_id=(2 * i + 1, j), device_id_type=MESH)

    @pl.when(c == 1)
    def _():
        def across(n, carry):
            pl.semaphore_signal(barrier, inc=1, device_id=(2 * i, n), device_id_type=MESH)
            return carry

        lax.fori_loop(0, 8, across, 0)


def relayout(block, st_ref, mask_ref):
    spread = jnp.concatenate([block[:, CHI * q : CHI * q + CHI] for q in range(CHI)], axis=0)
    high = spread.astype(jnp.bfloat16)
    rest = spread - high.astype(jnp.float32)
    mid = rest.astype(jnp.bfloat16)
    low = (rest - mid.astype(jnp.float32)).astype(jnp.bfloat16)
    st = st_ref[...]
    tiled = (
        jnp.dot(high, st, preferred_element_type=jnp.float32)
        + jnp.dot(mid, st, preferred_element_type=jnp.float32)
        + jnp.dot(low, st, preferred_element_type=jnp.float32)
    )
    return jnp.sum(tiled.reshape(CHI, CHI, PAIR) * mask_ref[...][None, :, :], axis=1)


def unit_of(part, kind, g, e):
    if part == 0:
        hi, lo = g, e
    elif part == 1:
        hi, lo = (2 * (g % 2) + e, g // 2) if kind else (2 * (g // 2) + e, g % 2)
    else:
        hi, lo = (g, e) if kind else (2 * (g // 2) + e, g % 2)
    return 6 * hi + 3 * lo + part


def second_place(part, kind, g, e):
    if part == 0:
        return 1 + e if kind else 3 * e
    half = (g % 2 if kind else 1 - g % 2) if part == 1 else (1 - g // 2 if kind else g // 2)
    return 2 * half + e


def owned_unit(part, g, m):
    if part == 0:
        kind = (m == 1) | (m == 2)
        return kind, jnp.where(kind, g, (g + 2 * m + 3) % 4)
    if part == 1:
        kind = m // 2 == g % 2
        return kind, jnp.where(kind, (2 * g + 3 * m + 2) % 4, 2 * (g // 2) + m % 2)
    kind = m // 2 != g // 2
    return kind, jnp.where(kind, 2 * (m % 2) + (m + 1) % 2, g % 2 + 2 * (m % 2))


def fused_kernel(
    t_ref, ps_ref, py_ref, eye_ref, st_ref, mask_ref, ox_ref, oy_ref,
    snd, got, zbuf, turned, m_up, m_low, q_ref,
    send_sem, recv_sem, fsend_sem, frecv_sem,
    parts1, parts2, parts3, sums1, sums2, mine, rows_ab, piece,
    s1_sem, r1_sem, s2_sem, r2_sem, s3_sem, r3_sem, out_sem, rows_sem, x_sem, rx_sem, y_sem, ry_sem,
    both_sem,
):
    i, c, j = place()
    here = coordinates()
    barrier = pltpu.get_barrier_semaphore()
    greet(i, c, j, barrier)

    def gather_unit(u, carry):
        rows = jnp.dot(ps_ref[...], t_ref[u], preferred_element_type=jnp.float32)
        rows = rows.astype(jnp.bfloat16)
        for h in range(2):
            for k in range(4):
                snd[u, :, 4 * h + k] = rows[
                    128 * h : 128 * h + 128, 128 * k : 128 * k + 128
                ].reshape(8, 16, 128)
        last = jnp.concatenate([rows[:128, 512:], rows[128:, 512:]], axis=1)
        snd[u, :, 8] = last.reshape(8, 16, 128)
        return carry

    lax.fori_loop(0, 12, gather_unit, 0)
    pl.when(c == 0)(lambda: pl.semaphore_wait(barrier, 71))
    pl.when(c == 1)(lambda: pl.semaphore_wait(barrier, 64))

    def send_unit(u, k, idest, jdest):
        x = 3 * i + (12 * c + u) // 8

        @pl.when(k > 0)
        def _():
            pltpu.make_async_remote_copy(
                src_ref=snd.at[u, jdest],
                dst_ref=got.at[x, j],
                send_sem=send_sem.at[u],
                recv_sem=recv_sem.at[k],
                device_id=(2 * idest + c, jdest),
                device_id_type=MESH,
            ).start()

        @pl.when(k == 0)
        def _():
            got[x, j] = snd[u, jdest]

    def send_to(k, carry):
        idest, jdest = partner(k, 1)
        first = (idest + 4 * c) % 8
        send_unit(first, k, idest, jdest)

        @pl.when(first < 4)
        def _():
            send_unit(first + 8, k, idest, jdest)

        return carry

    lax.fori_loop(0, 64, send_to, 0)

    two = (i < 4) == (c == 0)
    sibling = (2 * i + (1 - c), j)

    def forward(k, count, core):
        isrc, jsrc = partner(k, -1)
        x = 3 * isrc + jnp.where(core == 0, 0, 3 - count)
        ref = got.at[pl.ds(x, count), jsrc]
        return ref, pltpu.make_async_remote_copy(
            src_ref=ref,
            dst_ref=ref,
            send_sem=fsend_sem.at[k],
            recv_sem=frecv_sem.at[k],
            device_id=sibling,
            device_id_type=MESH,
        )

    def pass_on(k, carry):
        def one(count):
            ref, copy = forward(k, count, c)

            @pl.when(k > 0)
            def _():
                wait_for(ref, recv_sem.at[k])

            copy.start()

        pl.when(two)(lambda: one(2))
        pl.when(jnp.logical_not(two))(lambda: one(1))
        return carry

    def accept(k, carry):
        def one(count):
            forward(k, count, 1 - c)[1].wait_recv()

        pl.when(two)(lambda: one(1))
        pl.when(jnp.logical_not(two))(lambda: one(2))
        return carry

    def finish_forward(k, carry):
        def one(count):
            forward(k, count, c)[1].wait_send()

        pl.when(two)(lambda: one(2))
        pl.when(jnp.logical_not(two))(lambda: one(1))
        return carry

    def far(axis, parity, n):
        return (here[axis] + parity + 2 * n) % 4

    def stack_x(x, half):
        for n in range(2):
            js = pl.ds(2 * far(2, half, n), 2)
            for h in range(2):
                at = slice(64 * h + 32 * n, 64 * h + 32 * n + 32)
                for k in range(4):
                    zbuf[x, half, at, 128 * k : 128 * k + 128] = got[x, js, 4 * h + k].reshape(
                        32, 128
                    )
            last = got[x, js, 8].reshape(32, 128)
            zbuf[x, half, 32 * n : 32 * n + 32, 512:576] = last[:, :64]
            zbuf[x, half, 64 + 32 * n : 96 + 32 * n, 512:576] = last[:, 64:]

    def stack_y(jd, half):
        for n in range(2):
            xs = pl.ds(6 * far(0, half, n), 6)
            block = jnp.concatenate(
                [
                    jnp.concatenate(
                        [got[xs, jd, 4 * h + k].reshape(96, 128) for k in range(4)], axis=1
                    )
                    for h in range(2)
                ],
                axis=0,
            )
            rows = jnp.dot(py_ref[...], block, preferred_element_type=jnp.float32)
            last = got[xs, jd, 8].reshape(96, 128)
            tail = (
                jnp.dot(py_ref[:, :96], last, preferred_element_type=jnp.float32)[:, :64]
                + jnp.dot(py_ref[:, 96:], last, preferred_element_type=jnp.float32)[:, 64:]
            )
            rows = jnp.concatenate([rows, tail], axis=1).astype(jnp.bfloat16)
            for y in range(3):
                zbuf[3 * jd + y, half, 64 * n : 64 * n + 64] = rows[64 * y : 64 * y + 64]

    def turn(p, half):
        for w in range(2):
            for start, width in ((0, 256), (256, 256), (512, 64)):
                turned[w, start : start + width] = lax.dot_general(
                    eye_ref[:width, :width],
                    zbuf[2 * p + w, half, :, start : start + width],
                    NT,
                    preferred_element_type=jnp.float32,
                )
        rows_at = pl.ds(pl.multiple_of(48 * p, 16), 48)
        for z in range(24):
            cols = slice(128 * z, 128 * z + 128)
            straight = [turned[w, 24 * z : 24 * z + 24] for w in range(2)]
            m_up[half, rows_at, cols] = jnp.concatenate(straight, 0).astype(jnp.bfloat16)
            strided = [turned[w, pl.ds(z, 24, stride=24)] for w in range(2)]
            m_low[half, rows_at, cols] = jnp.concatenate(strided, 0).astype(jnp.bfloat16)

    def prepare(legs, half, meanwhile):
        for n in range(2):
            @pl.when(c == 0)
            def _(n=n):
                at = far(0, legs, n)

                def per_leg(m, carry):
                    stack_x(6 * at + m, half)
                    return carry

                lax.fori_loop(0, 6, per_leg, 0)

            @pl.when(c == 1)
            def _(n=n):
                at = far(2, legs, n)

                def per_leg(m, carry):
                    stack_y(2 * at + m, half)
                    return carry

                lax.fori_loop(0, 2, per_leg, 0)

            at = jnp.where(c == 0, far(0, legs, n), far(2, legs, n))

            def per_pair(m, carry):
                turn(3 * at + m, half)
                return carry

            lax.fori_loop(0, 3, per_pair, 0)
            meanwhile(n)

    panels = ((0, 256), (256, 256), (512, 64))

    def gram(which, m, half):
        base = PAIR * which
        for col, width in panels:
            total = lax.dot_general(
                m[half, col:, :1536], m[half, col : col + width, :1536],
                NT, preferred_element_type=jnp.float32,
            )
            total += lax.dot_general(
                m[half, col:, 1536:], m[half, col : col + width, 1536:],
                NT, preferred_element_type=jnp.float32,
            )
            if half:
                total += q_ref[base + col : base + PAIR, col : col + width]
            q_ref[base + col : base + PAIR, col : col + width] = total
            if half and col + width < PAIR:
                below = q_ref[base + col + width : base + PAIR, col : col + width]
                q_ref[base + col : base + col + width, col + width :] = below.T

    def passing(start, stop):
        lax.fori_loop(start, stop, pass_on, 0)

    def accepting(start, stop):
        lax.fori_loop(start, stop, accept, 0)

    passing(0, 16)
    accepting(0, 16)
    prepare(0, 0, lambda n: passing(16 + 8 * n, 24 + 8 * n))
    accepting(16, 32)

    @pl.when(c == 0)
    def _():
        prepare(0, 1, lambda n: passing(32 + 8 * n, 40 + 8 * n))

    @pl.when(c == 1)
    def _():
        prepare(1, 0, lambda n: passing(32 + 4 * n, 36 + 4 * n))
        gram(0, m_up, 0)
        passing(40, 44)
        gram(1, m_low, 0)
        passing(44, 48)

    accepting(32, 48)

    @pl.when(c == 0)
    def _():
        prepare(1, 0, lambda n: passing(48 + 4 * n, 52 + 4 * n))
        gram(0, m_up, 0)
        passing(56, 60)
        gram(1, m_low, 0)
        passing(60, 64)

    @pl.when(c == 1)
    def _():
        prepare(0, 1, lambda n: passing(48 + 8 * n, 56 + 8 * n))

    accepting(48, 64)
    prepare(1, 1, lambda n: None)

    scale = 1.0 / CHI**3

    def moved(axis, to):
        to_coords = [to if a == axis else here[a] for a in range(3)]
        di, dj = chip_at(*to_coords)
        return 2 * di + c, dj

    def axes(part):
        return part, (part + 1) % 3, (part + 2) % 3

    def stage1(which):
        for part in range(3):
            first = axes(part)[0]
            at = here[first]

            def rows(to, e, part=part):
                n = jnp.where(c == which, unit_of(part, 0, to, e), unit_of(part, 1, to, e))
                return pl.ds(pl.multiple_of(PAIR * which + CHI * n, 8), CHI)

            def send(step, carry, part=part, first=first, at=at, rows=rows):
                to = (at + step) % 4
                for e in range(2):
                    pltpu.make_async_remote_copy(
                        src_ref=q_ref.at[rows(to, e)],
                        dst_ref=parts1.at[part, which, at, e],
                        send_sem=s1_sem.at[part, which],
                        recv_sem=r1_sem.at[part, which],
                        device_id=moved(first, to),
                        device_id_type=MESH,
                    ).start()
                return carry

            lax.fori_loop(1, 4, send, 0)
            for e in range(2):
                parts1[part, which, at, e] = q_ref[rows(at, e)]

    def stage2(which):
        for part in range(3):
            first, second, _ = axes(part)
            g, at = here[first], here[second]
            ref = parts1.at[part, which]
            take(ref, 3, r1_sem.at[part, which])
            sums1[part, which] = (ref[0] + ref[1]) + (ref[2] + ref[3])
            for e in range(2):
                to = jnp.where(
                    c == which, second_place(part, 0, g, e), second_place(part, 1, g, e)
                )

                @pl.when(to != at)
                def _(part=part, second=second, at=at, to=to, e=e):
                    pltpu.make_async_remote_copy(
                        src_ref=sums1.at[part, which, e],
                        dst_ref=parts2.at[part, at],
                        send_sem=s2_sem.at[part],
                        recv_sem=r2_sem.at[part],
                        device_id=moved(second, to),
                        device_id_type=MESH,
                    ).start()

                @pl.when(to == at)
                def _(part=part, at=at, e=e):
                    parts2[part, at] = sums1[part, which, e]

    gram(0, m_up, 1)
    stage1(0)
    gram(1, m_low, 1)
    stage1(1)
    stage2(0)
    stage2(1)

    owner = []
    for part in range(3):
        first, second, third = axes(part)
        kind, to = owned_unit(part, here[first], here[second])
        at = here[third]
        owner.append((kind, to == at))
        take(parts2.at[part], 3, r2_sem.at[part])
        total = (parts2[part, 0] + parts2[part, 1]) + (parts2[part, 2] + parts2[part, 3])

        @pl.when(to == at)
        def _(part=part, at=at, total=total):
            parts3[part, at] = total

        @pl.when(to != at)
        def _(part=part, third=third, at=at, to=to, total=total):
            sums2[part] = total
            pltpu.make_async_remote_copy(
                src_ref=sums2.at[part],
                dst_ref=parts3.at[part, at],
                send_sem=s3_sem.at[part],
                recv_sem=r3_sem.at[part],
                device_id=moved(third, to),
                device_id_type=MESH,
            ).start()

    for part in range(3):
        kind, owns = owner[part]
        which = jnp.where(kind, 1 - c, c)

        @pl.when(owns)
        def _(part=part, kind=kind, which=which):
            take(parts3.at[part], 3, r3_sem.at[part])
            total = (parts3[part, 0] + parts3[part, 1]) + (parts3[part, 2] + parts3[part, 3])
            mine[part] = relayout(total * scale, st_ref, mask_ref)

            def give(step, carry):
                di = jnp.where(kind, (i + step) % 8, i)
                dj = jnp.where(kind, j, (j + step) % 8)
                pltpu.make_async_remote_copy(
                    src_ref=mine.at[part],
                    dst_ref=rows_ab.at[which, part],
                    send_sem=out_sem.at[part],
                    recv_sem=rows_sem.at[which, part],
                    device_id=(2 * di + c, dj),
                    device_id_type=MESH,
                ).start()
                return carry

            lax.fori_loop(1, 8, give, 0)
            rows_ab[which, part] = mine[part]

    for part in range(3):
        kind, owns = owner[part]
        for which in range(2):
            own = jnp.logical_and(owns, kind == (c != which))

            @pl.when(jnp.logical_not(own))
            def _(part=part, which=which):
                wait_for(rows_ab.at[which, part], rows_sem.at[which, part])

    product = lax.dot_general(
        rows_ab[0].reshape(72, PAIR), rows_ab[1].reshape(72, PAIR), NT,
        precision=HIGHEST, preferred_element_type=jnp.float32,
    ) * scale
    for a in range(3):
        piece[a] = product[CHI * a : CHI * a + CHI]

    def spread_x(first_two):
        for core in range(2):
            count = 2 if first_two == (core == 0) else 1
            start = 0 if core == 0 else 3 - count
            slot = 2 * j + (0 if core == 0 else 2 - count)
            source = piece.at[pl.ds(start, count)]
            target = ox_ref.at[pl.ds(slot, count)]

            def one(step, carry, core=core, source=source, target=target):
                pltpu.make_async_remote_copy(
                    src_ref=source,
                    dst_ref=target,
                    send_sem=x_sem.at[core],
                    recv_sem=rx_sem,
                    device_id=(2 * i + core, (j + step) % 8),
                    device_id_type=MESH,
                ).start()
                return carry

            lax.fori_loop(1 if core == 0 else 0, 8, one, 0)
            if core == 0:
                for a in range(count):
                    ox_ref[slot + a] = piece[start + a]

    swap = pltpu.make_async_remote_copy(
        src_ref=oy_ref,
        dst_ref=oy_ref,
        send_sem=both_sem.at[0],
        recv_sem=both_sem.at[1],
        device_id=(2 * i, j),
        device_id_type=MESH,
    )

    @pl.when(jnp.logical_and(c == 0, j < 4))
    def _():
        spread_x(True)

    @pl.when(jnp.logical_and(c == 0, j >= 4))
    def _():
        spread_x(False)

    @pl.when(c == 1)
    def _():
        def one(step, carry):
            pltpu.make_async_remote_copy(
                src_ref=piece,
                dst_ref=oy_ref.at[i],
                send_sem=y_sem,
                recv_sem=ry_sem,
                device_id=(2 * ((i + step) % 8) + 1, j),
                device_id_type=MESH,
            ).start()
            return carry

        lax.fori_loop(1, 8, one, 0)
        oy_ref[i] = piece[...]
        take(oy_ref, 7, ry_sem)
        swap.start()

    for part in range(3):
        for which in range(2):
            take(parts1.at[part, which], 3, s1_sem.at[part, which])
        take(parts2.at[part], 3, s2_sem.at[part])
        owns = owner[part][1]
        pl.when(jnp.logical_not(owns))(
            lambda part=part: wait_for(sums2.at[part], s3_sem.at[part])
        )
        pl.when(owns)(
            lambda part=part: wait_for(q_ref.at[pl.ds(0, 7 * CHI)], out_sem.at[part])
        )

    lax.fori_loop(0, 64, finish_forward, 0)

    def drain(u, carry):
        idest = (12 * c + u) % 8
        pl.when(idest == i)(lambda: take(snd.at[u], 7, send_sem.at[u]))
        pl.when(idest != i)(lambda: take(snd.at[u], 8, send_sem.at[u]))
        return carry

    lax.fori_loop(0, 12, drain, 0)

    @pl.when(jnp.logical_and(c == 0, j < 4))
    def _():
        take(ox_ref, 14, x_sem.at[0])
        take(ox_ref, 8, x_sem.at[1])
        take(ox_ref, 10, rx_sem)

    @pl.when(jnp.logical_and(c == 0, j >= 4))
    def _():
        take(ox_ref, 7, x_sem.at[0])
        take(ox_ref, 16, x_sem.at[1])
        take(ox_ref, 11, rx_sem)

    @pl.when(c == 0)
    def _():
        swap.wait_recv()

    @pl.when(c == 1)
    def _():
        take(ox_ref, 12, rx_sem)
        take(oy_ref, 7, y_sem)
        swap.wait_send()


def per_device(tensor, trial_x, trial_y):
    vmem = pl.BlockSpec(memory_space=pltpu.VMEM)
    dma = pltpu.SemaphoreType.DMA
    index = np.arange(PAIR)
    tile = (np.arange(CHI)[:, None] == index[None, :] % CHI).astype(np.float32)
    mask = (np.arange(CHI)[:, None] == index[None, :] // CHI).astype(np.float32)
    f32, bf16 = jnp.float32, jnp.bfloat16
    out_x, out_y = pl.pallas_call(
        fused_kernel,
        out_shape=[
            jax.ShapeDtypeStruct((16, CHI, 72), f32),
            jax.ShapeDtypeStruct((8, 3, CHI, 72), f32),
        ],
        in_specs=[vmem] * 6,
        out_specs=[vmem] * 2,
        scratch_shapes=[
            pltpu.VMEM((12, 8, 9, 16, 128), bf16),
            pltpu.VMEM((24, 8, 9, 16, 128), bf16),
            pltpu.VMEM((24, 2, 128, PAIR), bf16),
            pltpu.VMEM((2, PAIR, 128), f32),
            pltpu.VMEM((2, PAIR, 24 * 128), bf16),
            pltpu.VMEM((2, PAIR, 24 * 128), bf16),
            pltpu.VMEM((2 * PAIR, PAIR), f32),
            dma((12,)), dma((64,)), dma((64,)), dma((64,)),
            pltpu.VMEM((3, 2, 4, 2, CHI, PAIR), f32),
            pltpu.VMEM((3, 4, CHI, PAIR), f32),
            pltpu.VMEM((3, 4, CHI, PAIR), f32),
            pltpu.VMEM((3, 2, 2, CHI, PAIR), f32),
            pltpu.VMEM((3, CHI, PAIR), f32),
            pltpu.VMEM((3, CHI, PAIR), f32),
            pltpu.VMEM((2, 3, CHI, PAIR), f32),
            pltpu.VMEM((3, CHI, 72), f32),
            dma((3, 2)), dma((3, 2)), dma((3,)), dma((3,)), dma((3,)), dma((3,)),
            dma((3,)), dma((2, 3)), dma((2,)), dma, dma, dma, dma((2,)),
        ],
        compiler_params=pltpu.CompilerParams(
            collective_id=0, has_side_effects=True, vmem_limit_bytes=62 * 2**20
        ),
        name="hotrg_step",
    )(
        tensor.reshape(12, 216, PAIR),
        jnp.asarray(send_rows(), bf16),
        jnp.asarray(y_rows(), bf16),
        jnp.asarray(np.eye(256), bf16),
        jnp.asarray(tile, bf16),
        jnp.asarray(mask, f32),
    )

    core = lax.axis_index("aa") % 2
    rows_x = out_x.reshape(8, 2, CHI, 3, CHI).transpose(1, 0, 3, 2, 4).reshape(48, PAIR)
    gram_x = lax.dynamic_slice_in_dim(rows_x, core * 12, 36, 0)
    gram_y = out_y.reshape(8, 3, CHI, 3, CHI).transpose(1, 0, 3, 2, 4).reshape(72, PAIR)
    proj_x = jnp.dot(gram_x, trial_x, precision=HIGHEST, preferred_element_type=jnp.float32)
    proj_y = jnp.dot(gram_y, trial_y, precision=HIGHEST, preferred_element_type=jnp.float32)
    return (gram_x, proj_x, gram_y, proj_y)


def solution(mesh):
    in_specs = (P("aa", "ba", None), P(), P())
    out_specs = (P("aa", None), P("aa", None), P("ba", None), P("ba", None))
    return jax.shard_map(
        per_device, mesh=mesh, in_specs=in_specs, out_specs=out_specs, check_vma=False
    )
```

```python
import functools

import jax
import jax.numpy as jnp
import numpy as np
from jax import lax
from jax.experimental import pallas as pl
from jax.experimental.pallas import tpu as pltpu
from jax.sharding import PartitionSpec as P

CHI = 24
PAIR = 576
GROUPS = 8
MSG = 32
STACK = GROUPS * MSG
HIGHEST = lax.Precision.HIGHEST
MESH = pl.DeviceIdType.MESH
NT = (((1,), (1,)), ((), ()))


def send_rows():
    out = np.zeros((STACK, 216), np.float32)
    for jd in range(8):
        for xs in range(3):
            for y in range(3):
                for ys in range(3):
                    h, r = divmod(xs * 9 + y * 3 + ys, 16)
                    out[h * 128 + jd * 16 + r, xs * 72 + y * 24 + jd * 3 + ys] = 1
    return out


def y_rows():
    out = np.zeros((192, 192), np.float32)
    for xg in range(6):
        for xs in range(3):
            for y in range(3):
                for ys in range(3):
                    h, r = divmod(xs * 9 + y * 3 + ys, 16)
                    out[y * 64 + xg * 9 + xs * 3 + ys, h * 96 + xg * 16 + r] = 1
    return out


def place():
    aa = lax.axis_index("aa")
    ba = lax.axis_index("ba")
    return aa // 2, aa % 2, ba


def coordinates():
    aa = lax.axis_index("aa")
    ba = lax.axis_index("ba")
    return aa // 4, (aa // 2) % 2 + 2 * (ba % 2), ba // 2


def chip_at(z, x, y):
    return 2 * z + x % 2, 2 * y + x // 2


def shift_of(k):
    quarter, rest = k // 16, k % 16
    low, high = rest % 4, rest // 4
    dz = 2 * (low % 2) + quarter // 2
    dx = (low + high) % 4
    dy = 2 * ((high + low // 2) % 2) + quarter % 2
    return dz, dx, dy


def partner(k, sign):
    z, x, y = coordinates()
    dz, dx, dy = shift_of(k)
    return chip_at((z + 4 + sign * dz) % 4, (x + 4 + sign * dx) % 4, (y + 4 + sign * dy) % 4)


def wait_for(ref, sem):
    pltpu.make_async_copy(ref, ref, sem).wait()


def take(ref, count, sem):
    wait_for(ref.at[pl.ds(0, count)], sem)


def greet(i, c, j, barrier):
    def one(n, carry):
        di, dj = n // 8, n % 8

        @pl.when(jnp.logical_not(jnp.logical_and(di == i, dj == j)))
        def _():
            pl.semaphore_signal(barrier, inc=1, device_id=(2 * di + c, dj), device_id_type=MESH)

        return carry

    lax.fori_loop(0, 64, one, 0)

    @pl.when(c == 0)
    def _():
        pl.semaphore_signal(barrier, inc=1, device_id=(2 * i + 1, j), device_id_type=MESH)

    @pl.when(c == 1)
    def _():
        def across(n, carry):
            pl.semaphore_signal(barrier, inc=1, device_id=(2 * i, n), device_id_type=MESH)
            return carry

        lax.fori_loop(0, 8, across, 0)


def relayout(block, st_ref, mask_ref):
    high = block.astype(jnp.bfloat16).astype(jnp.float32)
    mid = (block - high).astype(jnp.bfloat16).astype(jnp.float32)
    terms = (high, mid, block - high - mid)
    spread = jnp.concatenate(
        [
            jnp.concatenate([term[:, CHI * q : CHI * q + CHI] for term in terms], axis=1)
            for q in range(CHI)
        ],
        axis=0,
    )
    tiled = jnp.dot(spread.astype(jnp.bfloat16), st_ref[...], preferred_element_type=jnp.float32)
    return jnp.sum(tiled.reshape(CHI, CHI, PAIR) * mask_ref[...][None, :, :], axis=1)


def unit_of(part, kind, g, e):
    if part == 0:
        hi, lo = g, e
    elif part == 1:
        hi, lo = (2 * (g % 2) + e, g // 2) if kind else (2 * (g // 2) + e, g % 2)
    else:
        hi, lo = (g, e) if kind else (2 * (g // 2) + e, g % 2)
    return 6 * hi + 3 * lo + part


def second_place(part, kind, g, e):
    if part == 0:
        return 1 + e if kind else 3 * e
    half = (g % 2 if kind else 1 - g % 2) if part == 1 else (1 - g // 2 if kind else g // 2)
    return 2 * half + e


def owned_unit(part, g, m):
    if part == 0:
        kind = (m == 1) | (m == 2)
        return kind, jnp.where(kind, g, (g + 2 * m + 3) % 4)
    if part == 1:
        kind = m // 2 == g % 2
        return kind, jnp.where(kind, (2 * g + 3 * m + 2) % 4, 2 * (g // 2) + m % 2)
    kind = m // 2 != g // 2
    return kind, jnp.where(kind, 2 * (m % 2) + (m + 1) % 2, g % 2 + 2 * (m % 2))


def fused_kernel(
    t_ref, ps_ref, py_ref, eye_ref, st_ref, mask_ref, ox_ref, oy_ref,
    snd, got, zbuf, turned, m_ref, q_ref,
    send_sem, recv_sem, fsend_sem, frecv_sem,
    parts1, parts2, parts3, sums1, sums2, mine, rows_ab, piece,
    s1_sem, r1_sem, s2_sem, r2_sem, s3_sem, r3_sem, out_sem, rows_sem, x_sem, rx_sem, y_sem, ry_sem,
    both_sem,
):
    i, c, j = place()
    here = coordinates()
    barrier = pltpu.get_barrier_semaphore()
    greet(i, c, j, barrier)

    def gather_unit(u, carry):
        rows = jnp.dot(ps_ref[...], t_ref[u], preferred_element_type=jnp.float32)
        rows = rows.astype(jnp.bfloat16)
        for h in range(2):
            for k in range(4):
                snd[u, :, 4 * h + k] = rows[
                    128 * h : 128 * h + 128, 128 * k : 128 * k + 128
                ].reshape(8, 16, 128)
        last = jnp.concatenate([rows[:128, 512:], rows[128:, 512:]], axis=1)
        snd[u, :, 8] = last.reshape(8, 16, 128)
        return carry

    lax.fori_loop(0, 12, gather_unit, 0)
    pl.when(c == 0)(lambda: pl.semaphore_wait(barrier, 71))
    pl.when(c == 1)(lambda: pl.semaphore_wait(barrier, 64))

    def send_unit(u, k, idest, jdest):
        x = 3 * i + (12 * c + u) // 8

        @pl.when(k > 0)
        def _():
            pltpu.make_async_remote_copy(
                src_ref=snd.at[u, jdest],
                dst_ref=got.at[x, j],
                send_sem=send_sem.at[u],
                recv_sem=recv_sem.at[k],
                device_id=(2 * idest + c, jdest),
                device_id_type=MESH,
            ).start()

        @pl.when(k == 0)
        def _():
            got[x, j] = snd[u, jdest]

    def send_to(k, carry):
        idest, jdest = partner(k, 1)
        first = (idest + 4 * c) % 8
        send_unit(first, k, idest, jdest)

        @pl.when(first < 4)
        def _():
            send_unit(first + 8, k, idest, jdest)

        return carry

    lax.fori_loop(0, 24, send_to, 0)

    two = (i < 4) == (c == 0)
    sibling = (2 * i + (1 - c), j)

    def forward(k, count, core):
        isrc, jsrc = partner(k, -1)
        x = 3 * isrc + jnp.where(core == 0, 0, 3 - count)
        ref = got.at[pl.ds(x, count), jsrc]
        return ref, pltpu.make_async_remote_copy(
            src_ref=ref,
            dst_ref=ref,
            send_sem=fsend_sem.at[k],
            recv_sem=frecv_sem.at[k],
            device_id=sibling,
            device_id_type=MESH,
        )

    def pass_on(k, carry):
        def one(count):
            ref, copy = forward(k, count, c)

            @pl.when(k > 0)
            def _():
                wait_for(ref, recv_sem.at[k])

            copy.start()

        pl.when(two)(lambda: one(2))
        pl.when(jnp.logical_not(two))(lambda: one(1))
        pl.when(k + 24 < 64)(lambda: send_to(k + 24, None))
        return carry

    def accept(k, carry):
        def one(count):
            forward(k, count, 1 - c)[1].wait_recv()

        pl.when(two)(lambda: one(1))
        pl.when(jnp.logical_not(two))(lambda: one(2))
        return carry

    def finish_forward(k, carry):
        def one(count):
            forward(k, count, c)[1].wait_send()

        pl.when(two)(lambda: one(2))
        pl.when(jnp.logical_not(two))(lambda: one(1))
        return carry

    def far(axis, parity, n):
        return (here[axis] + parity + 2 * n) % 4

    def stack_x(x, half):
        for n in range(2):
            js = pl.ds(2 * far(2, half, n), 2)
            for h in range(2):
                at = slice(64 * h + 32 * n, 64 * h + 32 * n + 32)
                for k in range(4):
                    zbuf[x, half, at, 128 * k : 128 * k + 128] = got[x, js, 4 * h + k].reshape(
                        32, 128
                    )
            last = got[x, js, 8].reshape(32, 128)
            zbuf[x, half, 32 * n : 32 * n + 32, 512:576] = last[:, :64]
            zbuf[x, half, 64 + 32 * n : 96 + 32 * n, 512:576] = last[:, 64:]

    def stack_y(jd, half):
        for n in range(2):
            xs = pl.ds(6 * far(0, half, n), 6)
            block = jnp.concatenate(
                [
                    jnp.concatenate(
                        [got[xs, jd, 4 * h + k].reshape(96, 128) for k in range(4)], axis=1
                    )
                    for h in range(2)
                ],
                axis=0,
            )
            rows = jnp.dot(py_ref[...], block, preferred_element_type=jnp.float32)
            last = got[xs, jd, 8].reshape(96, 128)
            tail = (
                jnp.dot(py_ref[:, :96], last, preferred_element_type=jnp.float32)[:, :64]
                + jnp.dot(py_ref[:, 96:], last, preferred_element_type=jnp.float32)[:, 64:]
            )
            rows = jnp.concatenate([rows, tail], axis=1).astype(jnp.bfloat16)
            for y in range(3):
                zbuf[3 * jd + y, half, 64 * n : 64 * n + 64] = rows[64 * y : 64 * y + 64]

    def turn(p, half):
        for w in range(2):
            for start, width in ((0, 256), (256, 256), (512, 64)):
                turned[w, start : start + width] = lax.dot_general(
                    eye_ref[:width, :width],
                    zbuf[2 * p + w, half, :, start : start + width],
                    NT,
                    preferred_element_type=jnp.float32,
                )
        rows_at = pl.ds(pl.multiple_of(48 * p, 16), 48)
        for z in range(24):
            cols = slice(128 * z, 128 * z + 128)
            straight = [turned[w, 24 * z : 24 * z + 24] for w in range(2)]
            m_ref[0, half, rows_at, cols] = jnp.concatenate(straight, 0).astype(jnp.bfloat16)
            strided = [turned[w, pl.ds(z, 24, stride=24)] for w in range(2)]
            m_ref[1, half, rows_at, cols] = jnp.concatenate(strided, 0).astype(jnp.bfloat16)

    scale = 1.0 / CHI**3

    def moved(axis, to):
        to_coords = [to if a == axis else here[a] for a in range(3)]
        di, dj = chip_at(*to_coords)
        return 2 * di + c, dj

    def axes(part):
        return part, (part + 1) % 3, (part + 2) % 3

    def stage1(which):
        for part in range(3):
            first = axes(part)[0]
            at = here[first]

            def rows(to, e, part=part):
                n = jnp.where(c == which, unit_of(part, 0, to, e), unit_of(part, 1, to, e))
                return pl.ds(pl.multiple_of(CHI * n, 8), CHI)

            def send(step, carry, part=part, first=first, at=at, rows=rows):
                to = (at + step) % 4
                for e in range(2):
                    pltpu.make_async_remote_copy(
                        src_ref=q_ref.at[which, rows(to, e)],
                        dst_ref=parts1.at[part, which, at, e],
                        send_sem=s1_sem.at[part, which],
                        recv_sem=r1_sem.at[part, which],
                        device_id=moved(first, to),
                        device_id_type=MESH,
                    ).start()
                return carry

            lax.fori_loop(1, 4, send, 0)
            for e in range(2):
                parts1[part, which, at, e] = q_ref[which, rows(at, e)]

    def passing(start, stop):
        lax.fori_loop(jnp.minimum(start, 64), jnp.minimum(stop, 64), pass_on, 0)

    def prepare(legs, half, ahead):
        def per_place(n, carry):
            at = jnp.where(c == 0, far(0, legs, n), far(2, legs, n))

            @pl.when(c == 0)
            def _():
                def per_leg(m, carry):
                    stack_x(6 * at + m, half)
                    return carry

                lax.fori_loop(0, 6, per_leg, 0)

            @pl.when(c == 1)
            def _():
                def per_leg(m, carry):
                    stack_y(2 * at + m, half)
                    return carry

                lax.fori_loop(0, 2, per_leg, 0)

            def per_pair(m, carry):
                turn(3 * at + m, half)
                return carry

            lax.fori_loop(0, 3, per_pair, 0)
            return carry

        lax.fori_loop(0, 2, per_place, 0)

    def gram(which, half):
        for col, width in ((0, 256), (256, 256), (512, 64)):
            before = q_ref[which, col:, col : col + width]
            total = jnp.where(half == 1, before, jnp.zeros_like(before))
            for ks in (slice(0, 1536), slice(1536, 3072)):
                total += lax.dot_general(
                    m_ref[which, half, col:, ks], m_ref[which, half, col : col + width, ks],
                    NT, preferred_element_type=jnp.float32,
                )
            q_ref[which, col:, col : col + width] = total

    def mirror(which):
        for col, width in ((0, 256), (256, 256)):
            below = q_ref[which, col + width :, col : col + width]
            q_ref[which, col : col + width, col + width :] = below.T

    passing(0, 16)

    def quarter(n, carry):
        ahead = 16 * n + 16
        lax.fori_loop(16 * n, ahead, accept, 0)
        near, distant = n % 2, n // 2
        legs = jnp.where(c == 0, distant, near)
        half = jnp.where(c == 0, near, distant)
        prepare(legs, half, ahead)
        last = n == 3
        multiplies = jnp.logical_or(last, n == 2 - c)

        @pl.when(multiplies)
        def _():
            def one(which, carry):
                gram(which, half)

                @pl.when(last)
                def _():
                    mirror(which)
                    stage1(which)

                return carry

            lax.fori_loop(0, 2, one, 0)

        passing(ahead, ahead + 16)
        return carry

    lax.fori_loop(0, 4, quarter, 0)

    def stage2(which):
        for part in range(3):
            first, second, _ = axes(part)
            g, at = here[first], here[second]
            ref = parts1.at[part, which]
            take(ref, 3, r1_sem.at[part, which])
            sums1[part, which] = (ref[0] + ref[1]) + (ref[2] + ref[3])
            for e in range(2):
                to = jnp.where(
                    c == which, second_place(part, 0, g, e), second_place(part, 1, g, e)
                )

                @pl.when(to != at)
                def _(part=part, second=second, at=at, to=to, e=e):
                    pltpu.make_async_remote_copy(
                        src_ref=sums1.at[part, which, e],
                        dst_ref=parts2.at[part, at],
                        send_sem=s2_sem.at[part],
                        recv_sem=r2_sem.at[part],
                        device_id=moved(second, to),
                        device_id_type=MESH,
                    ).start()

                @pl.when(to == at)
                def _(part=part, at=at, e=e):
                    parts2[part, at] = sums1[part, which, e]

    def both(which, carry):
        stage2(which)
        return carry

    lax.fori_loop(0, 2, both, 0)

    owner = []
    for part in range(3):
        first, second, third = axes(part)
        kind, to = owned_unit(part, here[first], here[second])
        at = here[third]
        owner.append((kind, to == at))
        take(parts2.at[part], 3, r2_sem.at[part])
        total = (parts2[part, 0] + parts2[part, 1]) + (parts2[part, 2] + parts2[part, 3])

        @pl.when(to == at)
        def _(part=part, at=at, total=total):
            parts3[part, at] = total

        @pl.when(to != at)
        def _(part=part, third=third, at=at, to=to, total=total):
            sums2[part] = total
            pltpu.make_async_remote_copy(
                src_ref=sums2.at[part],
                dst_ref=parts3.at[part, at],
                send_sem=s3_sem.at[part],
                recv_sem=r3_sem.at[part],
                device_id=moved(third, to),
                device_id_type=MESH,
            ).start()

    def own_part(part, carry):
        def pick(values):
            return jnp.where(part == 0, values[0], jnp.where(part == 1, values[1], values[2]))

        kind = pick([jnp.where(k, 1, 0) for k, _ in owner]) == 1
        owns = pick([jnp.where(o, 1, 0) for _, o in owner]) == 1
        which = jnp.where(kind, 1 - c, c)

        @pl.when(owns)
        def _():
            take(parts3.at[part], 3, r3_sem.at[part])
            total = (parts3[part, 0] + parts3[part, 1]) + (parts3[part, 2] + parts3[part, 3])
            mine[part] = relayout(total * scale, st_ref, mask_ref)

            def give(step, carry):
                di = jnp.where(kind, (i + step) % 8, i)
                dj = jnp.where(kind, j, (j + step) % 8)
                pltpu.make_async_remote_copy(
                    src_ref=mine.at[part],
                    dst_ref=rows_ab.at[which, part],
                    send_sem=out_sem.at[part],
                    recv_sem=rows_sem.at[which, part],
                    device_id=(2 * di + c, dj),
                    device_id_type=MESH,
                ).start()
                return carry

            lax.fori_loop(1, 8, give, 0)
            rows_ab[which, part] = mine[part]

        return carry

    lax.fori_loop(0, 3, own_part, 0)

    for part in range(3):
        kind, owns = owner[part]
        for which in range(2):
            own = jnp.logical_and(owns, kind == (c != which))

            @pl.when(jnp.logical_not(own))
            def _(part=part, which=which):
                wait_for(rows_ab.at[which, part], rows_sem.at[which, part])

    product = lax.dot_general(
        rows_ab[0].reshape(72, PAIR), rows_ab[1].reshape(72, PAIR), NT,
        precision=HIGHEST, preferred_element_type=jnp.float32,
    ) * scale
    for a in range(3):
        piece[a] = product[CHI * a : CHI * a + CHI]

    def spread_x(first_two):
        for core in range(2):
            count = 2 if first_two == (core == 0) else 1
            start = 0 if core == 0 else 3 - count
            slot = 2 * j + (0 if core == 0 else 2 - count)
            source = piece.at[pl.ds(start, count)]
            target = ox_ref.at[pl.ds(slot, count)]

            def one(step, carry, core=core, source=source, target=target):
                pltpu.make_async_remote_copy(
                    src_ref=source,
                    dst_ref=target,
                    send_sem=x_sem.at[core],
                    recv_sem=rx_sem,
                    device_id=(2 * i + core, (j + step) % 8),
                    device_id_type=MESH,
                ).start()
                return carry

            lax.fori_loop(1 if core == 0 else 0, 8, one, 0)
            if core == 0:
                for a in range(count):
                    ox_ref[slot + a] = piece[start + a]

    swap = pltpu.make_async_remote_copy(
        src_ref=oy_ref,
        dst_ref=oy_ref,
        send_sem=both_sem.at[0],
        recv_sem=both_sem.at[1],
        device_id=(2 * i, j),
        device_id_type=MESH,
    )

    @pl.when(jnp.logical_and(c == 0, j < 4))
    def _():
        spread_x(True)

    @pl.when(jnp.logical_and(c == 0, j >= 4))
    def _():
        spread_x(False)

    @pl.when(c == 1)
    def _():
        def one(step, carry):
            pltpu.make_async_remote_copy(
                src_ref=piece,
                dst_ref=oy_ref.at[i],
                send_sem=y_sem,
                recv_sem=ry_sem,
                device_id=(2 * ((i + step) % 8) + 1, j),
                device_id_type=MESH,
            ).start()
            return carry

        lax.fori_loop(1, 8, one, 0)
        oy_ref[i] = piece[...]
        take(oy_ref, 7, ry_sem)
        swap.start()

    for part in range(3):
        for which in range(2):
            take(parts1.at[part, which], 3, s1_sem.at[part, which])
        take(parts2.at[part], 3, s2_sem.at[part])
        owns = owner[part][1]
        pl.when(jnp.logical_not(owns))(
            lambda part=part: wait_for(sums2.at[part], s3_sem.at[part])
        )
        pl.when(owns)(
            lambda part=part: wait_for(q_ref.at[0, pl.ds(0, 7 * CHI)], out_sem.at[part])
        )

    lax.fori_loop(0, 64, finish_forward, 0)

    def drain(u, carry):
        idest = (12 * c + u) % 8
        pl.when(idest == i)(lambda: take(snd.at[u], 7, send_sem.at[u]))
        pl.when(idest != i)(lambda: take(snd.at[u], 8, send_sem.at[u]))
        return carry

    lax.fori_loop(0, 12, drain, 0)

    @pl.when(jnp.logical_and(c == 0, j < 4))
    def _():
        take(ox_ref, 14, x_sem.at[0])
        take(ox_ref, 8, x_sem.at[1])
        take(ox_ref, 10, rx_sem)

    @pl.when(jnp.logical_and(c == 0, j >= 4))
    def _():
        take(ox_ref, 7, x_sem.at[0])
        take(ox_ref, 16, x_sem.at[1])
        take(ox_ref, 11, rx_sem)

    @pl.when(c == 0)
    def _():
        swap.wait_recv()

    @pl.when(c == 1)
    def _():
        take(ox_ref, 12, rx_sem)
        take(oy_ref, 7, y_sem)
        swap.wait_send()


def per_device(tensor, trial_x, trial_y):
    vmem = pl.BlockSpec(memory_space=pltpu.VMEM)
    dma = pltpu.SemaphoreType.DMA
    index = np.arange(PAIR)
    tile = (np.arange(72)[:, None] % CHI == index[None, :] % CHI).astype(np.float32)
    mask = (np.arange(CHI)[:, None] == index[None, :] // CHI).astype(np.float32)
    f32, bf16 = jnp.float32, jnp.bfloat16
    out_x, out_y = pl.pallas_call(
        fused_kernel,
        out_shape=[
            jax.ShapeDtypeStruct((16, CHI, 72), f32),
            jax.ShapeDtypeStruct((8, 3, CHI, 72), f32),
        ],
        in_specs=[vmem] * 6,
        out_specs=[vmem] * 2,
        scratch_shapes=[
            pltpu.VMEM((12, 8, 9, 16, 128), bf16),
            pltpu.VMEM((24, 8, 9, 16, 128), bf16),
            pltpu.VMEM((24, 2, 128, PAIR), bf16),
            pltpu.VMEM((2, PAIR, 128), f32),
            pltpu.VMEM((2, 2, PAIR, 24 * 128), bf16),
            pltpu.VMEM((2, PAIR, PAIR), f32),
            dma((12,)), dma((64,)), dma((64,)), dma((64,)),
            pltpu.VMEM((3, 2, 4, 2, CHI, PAIR), f32),
            pltpu.VMEM((3, 4, CHI, PAIR), f32),
            pltpu.VMEM((3, 4, CHI, PAIR), f32),
            pltpu.VMEM((3, 2, 2, CHI, PAIR), f32),
            pltpu.VMEM((3, CHI, PAIR), f32),
            pltpu.VMEM((3, CHI, PAIR), f32),
            pltpu.VMEM((2, 3, CHI, PAIR), f32),
            pltpu.VMEM((3, CHI, 72), f32),
            dma((3, 2)), dma((3, 2)), dma((3,)), dma((3,)), dma((3,)), dma((3,)),
            dma((3,)), dma((2, 3)), dma((2,)), dma, dma, dma, dma((2,)),
        ],
        compiler_params=pltpu.CompilerParams(
            collective_id=0, has_side_effects=True, vmem_limit_bytes=62 * 2**20
        ),
        name="hotrg_step",
    )(
        tensor.reshape(12, 216, PAIR),
        jnp.asarray(send_rows(), bf16),
        jnp.asarray(y_rows(), bf16),
        jnp.asarray(np.eye(256), bf16),
        jnp.asarray(tile, bf16),
        jnp.asarray(mask, f32),
    )

    core = lax.axis_index("aa") % 2
    rows_x = out_x.reshape(8, 2, CHI, 3, CHI).transpose(1, 0, 3, 2, 4).reshape(48, PAIR)
    gram_x = lax.dynamic_slice_in_dim(rows_x, core * 12, 36, 0)
    gram_y = out_y.reshape(8, 3, CHI, 3, CHI).transpose(1, 0, 3, 2, 4).reshape(72, PAIR)
    proj_x = jnp.dot(gram_x, trial_x, precision=HIGHEST, preferred_element_type=jnp.float32)
    proj_y = jnp.dot(gram_y, trial_y, precision=HIGHEST, preferred_element_type=jnp.float32)
    return (gram_x, proj_x, gram_y, proj_y)


def solution(mesh):
    in_specs = (P("aa", "ba", None), P(), P())
    out_specs = (P("aa", None), P("aa", None), P("ba", None), P("ba", None))
    return jax.shard_map(
        per_device, mesh=mesh, in_specs=in_specs, out_specs=out_specs, check_vma=False
    )
```

```python
import functools

import jax
import jax.numpy as jnp
import numpy as np
from jax import lax
from jax.experimental import pallas as pl
from jax.experimental.pallas import tpu as pltpu
from jax.sharding import PartitionSpec as P

CHI = 24
PAIR = 576
GROUPS = 8
MSG = 32
STACK = GROUPS * MSG
HIGHEST = lax.Precision.HIGHEST
MESH = pl.DeviceIdType.MESH
NT = (((1,), (1,)), ((), ()))


def send_rows():
    out = np.zeros((STACK, 216), np.float32)
    for jd in range(8):
        for xs in range(3):
            for y in range(3):
                for ys in range(3):
                    h, r = divmod(xs * 9 + y * 3 + ys, 16)
                    out[h * 128 + jd * 16 + r, xs * 72 + y * 24 + jd * 3 + ys] = 1
    return out


def tail_slot(r):
    return (r % 14) // 5, 11 + (r % 14) % 5


def send_tails():
    out = np.zeros((2, 3, 8, 16, 216), np.float32)
    for jd in range(8):
        for xs in range(3):
            for y in range(3):
                for ys in range(3):
                    r = xs * 9 + y * 3 + ys
                    k, row = tail_slot(r)
                    out[r // 14, k, jd, row, xs * 72 + y * 24 + jd * 3 + ys] = 1
    return out.reshape(768, 216)


def x_tails():
    out = np.zeros((2, 2, 2, 16, 3, 2, 16), np.float32)
    for jj in range(2):
        for r in range(27):
            k, row = tail_slot(r)
            out[r // 14, r // 16, jj, r % 16, k, jj, row] = 1
    return out.reshape(128, 96)


def y_tails():
    out = np.zeros((2, 192, 3, 6, 16), np.float32)
    for xg in range(6):
        for xs in range(3):
            for y in range(3):
                for ys in range(3):
                    r = xs * 9 + y * 3 + ys
                    k, row = tail_slot(r)
                    out[r // 14, y * 64 + xg * 9 + xs * 3 + ys, k, xg, row] = 1
    return out.reshape(384, 288)


def y_rows():
    out = np.zeros((192, 192), np.float32)
    for xg in range(6):
        for xs in range(3):
            for y in range(3):
                for ys in range(3):
                    h, r = divmod(xs * 9 + y * 3 + ys, 16)
                    out[y * 64 + xg * 9 + xs * 3 + ys, h * 96 + xg * 16 + r] = 1
    return out


def place():
    aa = lax.axis_index("aa")
    ba = lax.axis_index("ba")
    return aa // 2, aa % 2, ba


def coordinates():
    aa = lax.axis_index("aa")
    ba = lax.axis_index("ba")
    return aa // 4, (aa // 2) % 2 + 2 * (ba % 2), ba // 2


def chip_at(z, x, y):
    return 2 * z + x % 2, 2 * y + x // 2


def shift_of(k):
    quarter, rest = k // 16, k % 16
    low, high = rest % 4, rest // 4
    dz = 2 * (low % 2) + quarter // 2
    dx = (low + high) % 4
    dy = 2 * ((high + low // 2) % 2) + quarter % 2
    return dz, dx, dy


def partner(k, sign):
    z, x, y = coordinates()
    dz, dx, dy = shift_of(k)
    return chip_at((z + 4 + sign * dz) % 4, (x + 4 + sign * dx) % 4, (y + 4 + sign * dy) % 4)


def wait_for(ref, sem):
    pltpu.make_async_copy(ref, ref, sem).wait()


def take(ref, count, sem):
    wait_for(ref.at[pl.ds(0, count)], sem)


def greet(i, c, j, barrier):
    def one(n, carry):
        di, dj = n // 8, n % 8

        @pl.when(jnp.logical_not(jnp.logical_and(di == i, dj == j)))
        def _():
            pl.semaphore_signal(barrier, inc=1, device_id=(2 * di + c, dj), device_id_type=MESH)

        return carry

    lax.fori_loop(0, 64, one, 0)

    @pl.when(c == 0)
    def _():
        pl.semaphore_signal(barrier, inc=1, device_id=(2 * i + 1, j), device_id_type=MESH)

    @pl.when(c == 1)
    def _():
        def across(n, carry):
            pl.semaphore_signal(barrier, inc=1, device_id=(2 * i, n), device_id_type=MESH)
            return carry

        lax.fori_loop(0, 8, across, 0)


def relayout(block, st_ref, mask_ref):
    high = block.astype(jnp.bfloat16).astype(jnp.float32)
    mid = (block - high).astype(jnp.bfloat16).astype(jnp.float32)
    terms = (high, mid, block - high - mid)
    spread = jnp.concatenate(
        [
            jnp.concatenate([term[:, CHI * q : CHI * q + CHI] for term in terms], axis=1)
            for q in range(CHI)
        ],
        axis=0,
    )
    tiled = jnp.dot(spread.astype(jnp.bfloat16), st_ref[...], preferred_element_type=jnp.float32)
    return jnp.sum(tiled.reshape(CHI, CHI, PAIR) * mask_ref[...][None, :, :], axis=1)


def unit_of(part, kind, g, e):
    if part == 0:
        hi, lo = g, e
    elif part == 1:
        hi, lo = (2 * (g % 2) + e, g // 2) if kind else (2 * (g // 2) + e, g % 2)
    else:
        hi, lo = (g, e) if kind else (2 * (g // 2) + e, g % 2)
    return 6 * hi + 3 * lo + part


def second_place(part, kind, g, e):
    if part == 0:
        return 1 + e if kind else 3 * e
    half = (g % 2 if kind else 1 - g % 2) if part == 1 else (1 - g // 2 if kind else g // 2)
    return 2 * half + e


def owned_unit(part, g, m):
    if part == 0:
        kind = (m == 1) | (m == 2)
        return kind, jnp.where(kind, g, (g + 2 * m + 3) % 4)
    if part == 1:
        kind = m // 2 == g % 2
        return kind, jnp.where(kind, (2 * g + 3 * m + 2) % 4, 2 * (g // 2) + m % 2)
    kind = m // 2 != g // 2
    return kind, jnp.where(kind, 2 * (m % 2) + (m + 1) % 2, g % 2 + 2 * (m % 2))


def fused_kernel(
    t_ref, ps_ref, pt_ref, py_ref, xt_ref, yt_ref, eye_ref, st_ref, mask_ref, ox_ref, oy_ref,
    unit, load_sem, snd, got, zbuf, turned, m_ref, q_ref,
    send_sem, recv_sem, fsend_sem, frecv_sem,
    parts1, parts2, parts3, sums1, sums2, mine, rows_ab, piece,
    s1_sem, r1_sem, s2_sem, r2_sem, s3_sem, r3_sem, out_sem, rows_sem, x_sem, rx_sem, y_sem, ry_sem,
    both_sem,
):
    i, c, j = place()
    here = coordinates()
    barrier = pltpu.get_barrier_semaphore()
    greet(i, c, j, barrier)

    def load(u):
        return pltpu.make_async_copy(t_ref.at[u], unit.at[u], load_sem.at[u])

    def start_load(u, carry):
        load(u).start()
        return carry

    lax.fori_loop(0, 12, start_load, 0)

    def gather_unit(u, carry):
        load(u).wait()
        rows = jnp.dot(ps_ref[...], unit[u], preferred_element_type=jnp.float32)
        ends = unit[u, :, 512:]
        ends = jnp.dot(
            pt_ref[...], jnp.concatenate([ends, ends], axis=1), preferred_element_type=jnp.float32
        )
        left = lax.broadcasted_iota(jnp.int32, (128, 128), 1) < 64
        for k in range(4):
            cols = slice(128 * k, 128 * k + 128)
            second = rows[128:, cols]
            if k < 3:
                at = 128 * k
                second += jnp.where(left, ends[at : at + 128], ends[384 + at : 512 + at])
            snd[u, :, k] = rows[:128, cols].astype(jnp.bfloat16).reshape(8, 16, 128)
            snd[u, :, 4 + k] = second.astype(jnp.bfloat16).reshape(8, 16, 128)
        return carry

    lax.fori_loop(0, 12, gather_unit, 0)
    pl.when(c == 0)(lambda: pl.semaphore_wait(barrier, 71))
    pl.when(c == 1)(lambda: pl.semaphore_wait(barrier, 64))

    def send_unit(u, k, idest, jdest):
        x = 3 * i + (12 * c + u) // 8

        @pl.when(k > 0)
        def _():
            pltpu.make_async_remote_copy(
                src_ref=snd.at[u, jdest],
                dst_ref=got.at[x, j],
                send_sem=send_sem.at[u],
                recv_sem=recv_sem.at[k],
                device_id=(2 * idest + c, jdest),
                device_id_type=MESH,
            ).start()

        @pl.when(k == 0)
        def _():
            got[x, j] = snd[u, jdest]

    def send_to(k, carry):
        idest, jdest = partner(k, 1)
        first = (idest + 4 * c) % 8
        send_unit(first, k, idest, jdest)

        @pl.when(first < 4)
        def _():
            send_unit(first + 8, k, idest, jdest)

        return carry

    lax.fori_loop(0, 16, send_to, 0)

    two = (i < 4) == (c == 0)
    sibling = (2 * i + (1 - c), j)

    def forward(k, count, core):
        isrc, jsrc = partner(k, -1)
        x = 3 * isrc + jnp.where(core == 0, 0, 3 - count)
        ref = got.at[pl.ds(x, count), jsrc]
        return ref, pltpu.make_async_remote_copy(
            src_ref=ref,
            dst_ref=ref,
            send_sem=fsend_sem.at[k],
            recv_sem=frecv_sem.at[k],
            device_id=sibling,
            device_id_type=MESH,
        )

    def pass_on(k, carry):
        def one(count):
            ref, copy = forward(k, count, c)

            @pl.when(k > 0)
            def _():
                wait_for(ref, recv_sem.at[k])

            copy.start()

        pl.when(two)(lambda: one(2))
        pl.when(jnp.logical_not(two))(lambda: one(1))
        pl.when(k + 16 < 64)(lambda: send_to(k + 16, None))
        return carry

    def accept(k, carry):
        def one(count):
            forward(k, count, 1 - c)[1].wait_recv()

        pl.when(two)(lambda: one(1))
        pl.when(jnp.logical_not(two))(lambda: one(2))
        return carry

    def finish_forward(k, carry):
        def one(count):
            forward(k, count, c)[1].wait_send()

        pl.when(two)(lambda: one(2))
        pl.when(jnp.logical_not(two))(lambda: one(1))
        return carry

    def far(axis, parity, n):
        return (here[axis] + parity + 2 * n) % 4

    def stack_x(x, half):
        for n in range(2):
            js = pl.ds(2 * far(2, half, n), 2)
            tails = jnp.concatenate([got[x, js, 4 + k].reshape(32, 128) for k in range(3)], axis=0)
            tails = jnp.dot(xt_ref[...], tails, preferred_element_type=jnp.float32)
            tails = (tails[:64, :64] + tails[64:, 64:]).astype(jnp.bfloat16)
            used = lax.broadcasted_iota(jnp.int32, (32, 128), 0) % 16 < 11
            for h in range(2):
                at = slice(64 * h + 32 * n, 64 * h + 32 * n + 32)
                for k in range(4):
                    block = got[x, js, 4 * h + k].reshape(32, 128)
                    if h:
                        block = jnp.where(used, block, jnp.zeros_like(block))
                    zbuf[x, half, at, 128 * k : 128 * k + 128] = block
                zbuf[x, half, at, 512:576] = tails[32 * h : 32 * h + 32]

    def stack_y(jd, half):
        for n in range(2):
            xs = pl.ds(6 * far(0, half, n), 6)
            block = jnp.concatenate(
                [
                    jnp.concatenate(
                        [got[xs, jd, 4 * h + k].reshape(96, 128) for k in range(4)], axis=1
                    )
                    for h in range(2)
                ],
                axis=0,
            )
            rows = jnp.dot(py_ref[...], block, preferred_element_type=jnp.float32)
            tails = jnp.concatenate([got[xs, jd, 4 + k].reshape(96, 128) for k in range(3)], axis=0)
            tails = jnp.dot(yt_ref[...], tails, preferred_element_type=jnp.float32)
            tail = tails[:192, :64] + tails[192:, 64:]
            rows = jnp.concatenate([rows, tail], axis=1).astype(jnp.bfloat16)
            for y in range(3):
                zbuf[3 * jd + y, half, 64 * n : 64 * n + 64] = rows[64 * y : 64 * y + 64]

    def turn(p, half):
        for w in range(2):
            for start, width in ((0, 256), (256, 256), (512, 64)):
                turned[w, start : start + width] = lax.dot_general(
                    eye_ref[:width, :width],
                    zbuf[2 * p + w, half, :, start : start + width],
                    NT,
                    preferred_element_type=jnp.float32,
                )
        rows_at = pl.ds(pl.multiple_of(48 * p, 16), 48)
        for z in range(24):
            cols = slice(128 * z, 128 * z + 128)
            straight = [turned[w, 24 * z : 24 * z + 24] for w in range(2)]
            m_ref[0, half, rows_at, cols] = jnp.concatenate(straight, 0).astype(jnp.bfloat16)
            strided = [turned[w, pl.ds(z, 24, stride=24)] for w in range(2)]
            m_ref[1, half, rows_at, cols] = jnp.concatenate(strided, 0).astype(jnp.bfloat16)

    scale = 1.0 / CHI**3

    def moved(axis, to):
        to_coords = [to if a == axis else here[a] for a in range(3)]
        di, dj = chip_at(*to_coords)
        return 2 * di + c, dj

    def axes(part):
        return part, (part + 1) % 3, (part + 2) % 3

    def stage1(which):
        for part in range(3):
            first = axes(part)[0]
            at = here[first]

            def rows(to, e, part=part):
                n = jnp.where(c == which, unit_of(part, 0, to, e), unit_of(part, 1, to, e))
                return pl.ds(pl.multiple_of(CHI * n, 8), CHI)

            def send(step, carry, part=part, first=first, at=at, rows=rows):
                to = (at + step) % 4
                for e in range(2):
                    pltpu.make_async_remote_copy(
                        src_ref=q_ref.at[which, rows(to, e)],
                        dst_ref=parts1.at[part, which, at, e],
                        send_sem=s1_sem.at[part, which],
                        recv_sem=r1_sem.at[part, which],
                        device_id=moved(first, to),
                        device_id_type=MESH,
                    ).start()
                return carry

            lax.fori_loop(1, 4, send, 0)
            for e in range(2):
                parts1[part, which, at, e] = q_ref[which, rows(at, e)]

    def passing(start, stop):
        lax.fori_loop(jnp.minimum(start, 64), jnp.minimum(stop, 64), pass_on, 0)

    def prepare(legs, half, ahead):
        def per_place(n, carry):
            at = jnp.where(c == 0, far(0, legs, n), far(2, legs, n))

            @pl.when(c == 0)
            def _():
                def per_leg(m, carry):
                    stack_x(6 * at + m, half)
                    return carry

                lax.fori_loop(0, 6, per_leg, 0)

            @pl.when(c == 1)
            def _():
                def per_leg(m, carry):
                    stack_y(2 * at + m, half)
                    return carry

                lax.fori_loop(0, 2, per_leg, 0)

            def per_pair(m, carry):
                turn(3 * at + m, half)
                return carry

            lax.fori_loop(0, 3, per_pair, 0)
            return carry

        lax.fori_loop(0, 2, per_place, 0)

    def gram(which, half):
        for col, width in ((0, 256), (256, 256), (512, 64)):
            before = q_ref[which, col:, col : col + width]
            total = jnp.where(half == 1, before, jnp.zeros_like(before))
            for ks in (slice(0, 1536), slice(1536, 3072)):
                total += lax.dot_general(
                    m_ref[which, half, col:, ks], m_ref[which, half, col : col + width, ks],
                    NT, preferred_element_type=jnp.float32,
                )
            q_ref[which, col:, col : col + width] = total

    def mirror(which):
        for col, width in ((0, 256), (256, 256)):
            below = q_ref[which, col + width :, col : col + width]
            q_ref[which, col : col + width, col + width :] = below.T

    passing(0, 16)

    def quarter(n, carry):
        ahead = 16 * n + 16
        lax.fori_loop(16 * n, ahead, accept, 0)
        near, distant = n % 2, n // 2
        legs = jnp.where(c == 0, distant, near)
        half = jnp.where(c == 0, near, distant)
        prepare(legs, half, ahead)
        last = n == 3
        multiplies = jnp.logical_or(last, n == 2 - c)

        @pl.when(multiplies)
        def _():
            def one(which, carry):
                gram(which, half)

                @pl.when(last)
                def _():
                    mirror(which)
                    stage1(which)

                return carry

            lax.fori_loop(0, 2, one, 0)

        passing(ahead, ahead + 16)
        return carry

    lax.fori_loop(0, 4, quarter, 0)

    def stage2(which):
        for part in range(3):
            first, second, _ = axes(part)
            g, at = here[first], here[second]
            ref = parts1.at[part, which]
            take(ref, 3, r1_sem.at[part, which])
            sums1[part, which] = (ref[0] + ref[1]) + (ref[2] + ref[3])
            for e in range(2):
                to = jnp.where(
                    c == which, second_place(part, 0, g, e), second_place(part, 1, g, e)
                )

                @pl.when(to != at)
                def _(part=part, second=second, at=at, to=to, e=e):
                    pltpu.make_async_remote_copy(
                        src_ref=sums1.at[part, which, e],
                        dst_ref=parts2.at[part, at],
                        send_sem=s2_sem.at[part],
                        recv_sem=r2_sem.at[part],
                        device_id=moved(second, to),
                        device_id_type=MESH,
                    ).start()

                @pl.when(to == at)
                def _(part=part, at=at, e=e):
                    parts2[part, at] = sums1[part, which, e]

    def both(which, carry):
        stage2(which)
        return carry

    lax.fori_loop(0, 2, both, 0)

    owner = []
    for part in range(3):
        first, second, third = axes(part)
        kind, to = owned_unit(part, here[first], here[second])
        at = here[third]
        owner.append((kind, to == at))
        take(parts2.at[part], 3, r2_sem.at[part])
        total = (parts2[part, 0] + parts2[part, 1]) + (parts2[part, 2] + parts2[part, 3])

        @pl.when(to == at)
        def _(part=part, at=at, total=total):
            parts3[part, at] = total

        @pl.when(to != at)
        def _(part=part, third=third, at=at, to=to, total=total):
            sums2[part] = total
            pltpu.make_async_remote_copy(
                src_ref=sums2.at[part],
                dst_ref=parts3.at[part, at],
                send_sem=s3_sem.at[part],
                recv_sem=r3_sem.at[part],
                device_id=moved(third, to),
                device_id_type=MESH,
            ).start()

    def own_part(part, carry):
        def pick(values):
            return jnp.where(part == 0, values[0], jnp.where(part == 1, values[1], values[2]))

        kind = pick([jnp.where(k, 1, 0) for k, _ in owner]) == 1
        owns = pick([jnp.where(o, 1, 0) for _, o in owner]) == 1
        which = jnp.where(kind, 1 - c, c)

        @pl.when(owns)
        def _():
            take(parts3.at[part], 3, r3_sem.at[part])
            total = (parts3[part, 0] + parts3[part, 1]) + (parts3[part, 2] + parts3[part, 3])
            mine[part] = relayout(total * scale, st_ref, mask_ref)

            def give(step, carry):
                di = jnp.where(kind, (i + step) % 8, i)
                dj = jnp.where(kind, j, (j + step) % 8)
                pltpu.make_async_remote_copy(
                    src_ref=mine.at[part],
                    dst_ref=rows_ab.at[which, part],
                    send_sem=out_sem.at[part],
                    recv_sem=rows_sem.at[which, part],
                    device_id=(2 * di + c, dj),
                    device_id_type=MESH,
                ).start()
                return carry

            lax.fori_loop(1, 8, give, 0)
            rows_ab[which, part] = mine[part]

        return carry

    lax.fori_loop(0, 3, own_part, 0)

    for part in range(3):
        kind, owns = owner[part]
        for which in range(2):
            own = jnp.logical_and(owns, kind == (c != which))

            @pl.when(jnp.logical_not(own))
            def _(part=part, which=which):
                wait_for(rows_ab.at[which, part], rows_sem.at[which, part])

    product = lax.dot_general(
        rows_ab[0].reshape(72, PAIR), rows_ab[1].reshape(72, PAIR), NT,
        precision=HIGHEST, preferred_element_type=jnp.float32,
    ) * scale
    for a in range(3):
        piece[a] = product[CHI * a : CHI * a + CHI]

    def spread_x(first_two):
        for core in range(2):
            count = 2 if first_two == (core == 0) else 1
            start = 0 if core == 0 else 3 - count
            slot = 2 * j + (0 if core == 0 else 2 - count)
            source = piece.at[pl.ds(start, count)]
            target = ox_ref.at[pl.ds(slot, count)]

            def one(step, carry, core=core, source=source, target=target):
                pltpu.make_async_remote_copy(
                    src_ref=source,
                    dst_ref=target,
                    send_sem=x_sem.at[core],
                    recv_sem=rx_sem,
                    device_id=(2 * i + core, (j + step) % 8),
                    device_id_type=MESH,
                ).start()
                return carry

            lax.fori_loop(1 if core == 0 else 0, 8, one, 0)
            if core == 0:
                for a in range(count):
                    ox_ref[slot + a] = piece[start + a]

    swap = pltpu.make_async_remote_copy(
        src_ref=oy_ref,
        dst_ref=oy_ref,
        send_sem=both_sem.at[0],
        recv_sem=both_sem.at[1],
        device_id=(2 * i, j),
        device_id_type=MESH,
    )

    @pl.when(jnp.logical_and(c == 0, j < 4))
    def _():
        spread_x(True)

    @pl.when(jnp.logical_and(c == 0, j >= 4))
    def _():
        spread_x(False)

    @pl.when(c == 1)
    def _():
        def one(step, carry):
            pltpu.make_async_remote_copy(
                src_ref=piece,
                dst_ref=oy_ref.at[i],
                send_sem=y_sem,
                recv_sem=ry_sem,
                device_id=(2 * ((i + step) % 8) + 1, j),
                device_id_type=MESH,
            ).start()
            return carry

        lax.fori_loop(1, 8, one, 0)
        oy_ref[i] = piece[...]
        take(oy_ref, 7, ry_sem)
        swap.start()

    for part in range(3):
        for which in range(2):
            take(parts1.at[part, which], 3, s1_sem.at[part, which])
        take(parts2.at[part], 3, s2_sem.at[part])
        owns = owner[part][1]
        pl.when(jnp.logical_not(owns))(
            lambda part=part: wait_for(sums2.at[part], s3_sem.at[part])
        )
        pl.when(owns)(
            lambda part=part: wait_for(q_ref.at[0, pl.ds(0, 7 * CHI)], out_sem.at[part])
        )

    lax.fori_loop(0, 64, finish_forward, 0)

    def drain(u, carry):
        idest = (12 * c + u) % 8
        pl.when(idest == i)(lambda: take(snd.at[u], 7, send_sem.at[u]))
        pl.when(idest != i)(lambda: take(snd.at[u], 8, send_sem.at[u]))
        return carry

    lax.fori_loop(0, 12, drain, 0)

    @pl.when(jnp.logical_and(c == 0, j < 4))
    def _():
        take(ox_ref, 14, x_sem.at[0])
        take(ox_ref, 8, x_sem.at[1])
        take(ox_ref, 10, rx_sem)

    @pl.when(jnp.logical_and(c == 0, j >= 4))
    def _():
        take(ox_ref, 7, x_sem.at[0])
        take(ox_ref, 16, x_sem.at[1])
        take(ox_ref, 11, rx_sem)

    @pl.when(c == 0)
    def _():
        swap.wait_recv()

    @pl.when(c == 1)
    def _():
        take(ox_ref, 12, rx_sem)
        take(oy_ref, 7, y_sem)
        swap.wait_send()


def per_device(tensor, trial_x, trial_y):
    vmem = pl.BlockSpec(memory_space=pltpu.VMEM)
    dma = pltpu.SemaphoreType.DMA
    index = np.arange(PAIR)
    tile = (np.arange(72)[:, None] % CHI == index[None, :] % CHI).astype(np.float32)
    mask = (np.arange(CHI)[:, None] == index[None, :] // CHI).astype(np.float32)
    f32, bf16 = jnp.float32, jnp.bfloat16
    out_x, out_y = pl.pallas_call(
        fused_kernel,
        out_shape=[
            jax.ShapeDtypeStruct((16, CHI, 72), f32),
            jax.ShapeDtypeStruct((8, 3, CHI, 72), f32),
        ],
        in_specs=[pl.BlockSpec(memory_space=pl.ANY)] + [vmem] * 8,
        out_specs=[vmem] * 2,
        scratch_shapes=[
            pltpu.VMEM((12, 216, PAIR), bf16),
            dma((12,)),
            pltpu.VMEM((12, 8, 8, 16, 128), bf16),
            pltpu.VMEM((24, 8, 8, 16, 128), bf16),
            pltpu.VMEM((24, 2, 128, PAIR), bf16),
            pltpu.VMEM((2, PAIR, 128), f32),
            pltpu.VMEM((2, 2, PAIR, 24 * 128), bf16),
            pltpu.VMEM((2, PAIR, PAIR), f32),
            dma((12,)), dma((64,)), dma((64,)), dma((64,)),
            pltpu.VMEM((3, 2, 4, 2, CHI, PAIR), f32),
            pltpu.VMEM((3, 4, CHI, PAIR), f32),
            pltpu.VMEM((3, 4, CHI, PAIR), f32),
            pltpu.VMEM((3, 2, 2, CHI, PAIR), f32),
            pltpu.VMEM((3, CHI, PAIR), f32),
            pltpu.VMEM((3, CHI, PAIR), f32),
            pltpu.VMEM((2, 3, CHI, PAIR), f32),
            pltpu.VMEM((3, CHI, 72), f32),
            dma((3, 2)), dma((3, 2)), dma((3,)), dma((3,)), dma((3,)), dma((3,)),
            dma((3,)), dma((2, 3)), dma((2,)), dma, dma, dma, dma((2,)),
        ],
        compiler_params=pltpu.CompilerParams(
            collective_id=0, has_side_effects=True, vmem_limit_bytes=62 * 2**20
        ),
        name="hotrg_step",
    )(
        tensor.reshape(12, 216, PAIR),
        jnp.asarray(send_rows(), bf16),
        jnp.asarray(send_tails(), bf16),
        jnp.asarray(y_rows(), bf16),
        jnp.asarray(x_tails(), bf16),
        jnp.asarray(y_tails(), bf16),
        jnp.asarray(np.eye(256), bf16),
        jnp.asarray(tile, bf16),
        jnp.asarray(mask, f32),
    )

    core = lax.axis_index("aa") % 2
    rows_x = out_x.reshape(8, 2, CHI, 3, CHI).transpose(1, 0, 3, 2, 4).reshape(48, PAIR)
    gram_x = lax.dynamic_slice_in_dim(rows_x, core * 12, 36, 0)
    gram_y = out_y.reshape(8, 3, CHI, 3, CHI).transpose(1, 0, 3, 2, 4).reshape(72, PAIR)
    proj_x = jnp.dot(gram_x, trial_x, precision=HIGHEST, preferred_element_type=jnp.float32)
    proj_y = jnp.dot(gram_y, trial_y, precision=HIGHEST, preferred_element_type=jnp.float32)
    return (gram_x, proj_x, gram_y, proj_y)


def solution(mesh):
    in_specs = (P("aa", "ba", None), P(), P())
    out_specs = (P("aa", None), P("aa", None), P("ba", None), P("ba", None))
    return jax.shard_map(
        per_device, mesh=mesh, in_specs=in_specs, out_specs=out_specs, check_vma=False
    )
```

```python
import functools

import jax
import jax.numpy as jnp
import numpy as np
from jax import lax
from jax.experimental import pallas as pl
from jax.experimental.pallas import tpu as pltpu
from jax.sharding import PartitionSpec as P

CHI = 24
PAIR = 576
GROUPS = 8
MSG = 32
STACK = GROUPS * MSG
HIGHEST = lax.Precision.HIGHEST
MESH = pl.DeviceIdType.MESH
NT = (((1,), (1,)), ((), ()))


def send_rows():
    out = np.zeros((STACK, 216), np.float32)
    for jd in range(8):
        for xs in range(3):
            for y in range(3):
                for ys in range(3):
                    h, r = divmod(xs * 9 + y * 3 + ys, 16)
                    out[h * 128 + jd * 16 + r, xs * 72 + y * 24 + jd * 3 + ys] = 1
    return out


def tail_slot(r):
    return (r % 14) // 5, 11 + (r % 14) % 5


def send_tails():
    out = np.zeros((2, 3, 8, 16, 216), np.float32)
    for jd in range(8):
        for xs in range(3):
            for y in range(3):
                for ys in range(3):
                    r = xs * 9 + y * 3 + ys
                    k, row = tail_slot(r)
                    out[r // 14, k, jd, row, xs * 72 + y * 24 + jd * 3 + ys] = 1
    return out.reshape(768, 216)


def x_tails():
    out = np.zeros((2, 2, 2, 16, 3, 2, 16), np.float32)
    for jj in range(2):
        for r in range(27):
            k, row = tail_slot(r)
            out[r // 14, r // 16, jj, r % 16, k, jj, row] = 1
    return out.reshape(128, 96)


def y_tails():
    out = np.zeros((2, 192, 3, 6, 16), np.float32)
    for xg in range(6):
        for xs in range(3):
            for y in range(3):
                for ys in range(3):
                    r = xs * 9 + y * 3 + ys
                    k, row = tail_slot(r)
                    out[r // 14, y * 64 + xg * 9 + xs * 3 + ys, k, xg, row] = 1
    return out.reshape(384, 288)


def y_rows():
    out = np.zeros((192, 192), np.float32)
    for xg in range(6):
        for xs in range(3):
            for y in range(3):
                for ys in range(3):
                    h, r = divmod(xs * 9 + y * 3 + ys, 16)
                    out[y * 64 + xg * 9 + xs * 3 + ys, h * 96 + xg * 16 + r] = 1
    return out


def place():
    aa = lax.axis_index("aa")
    ba = lax.axis_index("ba")
    return aa // 2, aa % 2, ba


def coordinates():
    aa = lax.axis_index("aa")
    ba = lax.axis_index("ba")
    return aa // 4, (aa // 2) % 2 + 2 * (ba % 2), ba // 2


def chip_at(z, x, y):
    return 2 * z + x % 2, 2 * y + x // 2


def shift_of(k):
    quarter, rest = k // 16, k % 16
    low, high = rest % 4, rest // 4
    dz = 2 * (low % 2) + quarter // 2
    dx = (low + high) % 4
    dy = 2 * ((high + low // 2) % 2) + quarter % 2
    return dz, dx, dy


def partner(k, sign):
    z, x, y = coordinates()
    dz, dx, dy = shift_of(k)
    return chip_at((z + 4 + sign * dz) % 4, (x + 4 + sign * dx) % 4, (y + 4 + sign * dy) % 4)


def wait_for(ref, sem):
    pltpu.make_async_copy(ref, ref, sem).wait()


def take(ref, count, sem):
    wait_for(ref.at[pl.ds(0, count)], sem)


def greet(i, c, j, barrier):
    def one(n, carry):
        di, dj = n // 8, n % 8

        @pl.when(jnp.logical_not(jnp.logical_and(di == i, dj == j)))
        def _():
            pl.semaphore_signal(barrier, inc=1, device_id=(2 * di + c, dj), device_id_type=MESH)

        return carry

    lax.fori_loop(0, 64, one, 0)

    @pl.when(c == 0)
    def _():
        pl.semaphore_signal(barrier, inc=1, device_id=(2 * i + 1, j), device_id_type=MESH)

    @pl.when(c == 1)
    def _():
        def across(n, carry):
            pl.semaphore_signal(barrier, inc=1, device_id=(2 * i, n), device_id_type=MESH)
            return carry

        lax.fori_loop(0, 8, across, 0)


def relayout(block, st_ref, mask_ref):
    high = block.astype(jnp.bfloat16).astype(jnp.float32)
    mid = (block - high).astype(jnp.bfloat16).astype(jnp.float32)
    terms = (high, mid, block - high - mid)
    spread = jnp.concatenate(
        [
            jnp.concatenate([term[:, CHI * q : CHI * q + CHI] for term in terms], axis=1)
            for q in range(CHI)
        ],
        axis=0,
    )
    tiled = jnp.dot(spread.astype(jnp.bfloat16), st_ref[...], preferred_element_type=jnp.float32)
    return jnp.sum(tiled.reshape(CHI, CHI, PAIR) * mask_ref[...][None, :, :], axis=1)


def unit_of(part, kind, g, e):
    if part == 0:
        hi, lo = g, e
    elif part == 1:
        hi, lo = (2 * (g % 2) + e, g // 2) if kind else (2 * (g // 2) + e, g % 2)
    else:
        hi, lo = (g, e) if kind else (2 * (g // 2) + e, g % 2)
    return 6 * hi + 3 * lo + part


def second_place(part, kind, g, e):
    if part == 0:
        return 1 + e if kind else 3 * e
    half = (g % 2 if kind else 1 - g % 2) if part == 1 else (1 - g // 2 if kind else g // 2)
    return 2 * half + e


def owned_unit(part, g, m):
    if part == 0:
        kind = (m == 1) | (m == 2)
        return kind, jnp.where(kind, g, (g + 2 * m + 3) % 4)
    if part == 1:
        kind = m // 2 == g % 2
        return kind, jnp.where(kind, (2 * g + 3 * m + 2) % 4, 2 * (g // 2) + m % 2)
    kind = m // 2 != g // 2
    return kind, jnp.where(kind, 2 * (m % 2) + (m + 1) % 2, g % 2 + 2 * (m % 2))


def fused_kernel(
    t_ref, ps_ref, pt_ref, py_ref, xt_ref, yt_ref, eye_ref, st_ref, mask_ref, ox_ref, oy_ref,
    unit, load_sem, snd, got, zbuf, turned, m_ref, q_ref,
    send_sem, recv_sem, fsend_sem, frecv_sem,
    parts1, parts2, parts3, sums1, sums2, mine, rows_ab, piece,
    s1_sem, r1_sem, s2_sem, r2_sem, s3_sem, r3_sem, out_sem, rows_sem, x_sem, rx_sem, y_sem, ry_sem,
    both_sem,
):
    i, c, j = place()
    here = coordinates()
    barrier = pltpu.get_barrier_semaphore()
    greet(i, c, j, barrier)

    def load(u):
        return pltpu.make_async_copy(t_ref.at[u], unit.at[u], load_sem.at[u])

    def start_load(u, carry):
        load(u).start()
        return carry

    lax.fori_loop(0, 12, start_load, 0)

    def gather_unit(u, carry):
        load(u).wait()
        rows = jnp.dot(ps_ref[...], unit[u], preferred_element_type=jnp.float32)
        ends = unit[u, :, 512:]
        ends = jnp.dot(
            pt_ref[...], jnp.concatenate([ends, ends], axis=1), preferred_element_type=jnp.float32
        )
        left = lax.broadcasted_iota(jnp.int32, (128, 128), 1) < 64
        for k in range(4):
            cols = slice(128 * k, 128 * k + 128)
            second = rows[128:, cols]
            if k < 3:
                at = 128 * k
                second += jnp.where(left, ends[at : at + 128], ends[384 + at : 512 + at])
            snd[u, :, k] = rows[:128, cols].astype(jnp.bfloat16).reshape(8, 16, 128)
            snd[u, :, 4 + k] = second.astype(jnp.bfloat16).reshape(8, 16, 128)
        return carry

    lax.fori_loop(0, 12, gather_unit, 0)
    pl.when(c == 0)(lambda: pl.semaphore_wait(barrier, 71))
    pl.when(c == 1)(lambda: pl.semaphore_wait(barrier, 64))

    def send_unit(u, k, idest, jdest):
        x = 3 * i + (12 * c + u) // 8

        @pl.when(k > 0)
        def _():
            pltpu.make_async_remote_copy(
                src_ref=snd.at[u, jdest],
                dst_ref=got.at[x, j],
                send_sem=send_sem.at[u],
                recv_sem=recv_sem.at[k],
                device_id=(2 * idest + c, jdest),
                device_id_type=MESH,
            ).start()

        @pl.when(k == 0)
        def _():
            got[x, j] = snd[u, jdest]

    def send_to(k, carry):
        idest, jdest = partner(k, 1)
        first = (idest + 4 * c) % 8
        send_unit(first, k, idest, jdest)

        @pl.when(first < 4)
        def _():
            send_unit(first + 8, k, idest, jdest)

        return carry

    lax.fori_loop(0, 16, send_to, 0)

    two = (i < 4) == (c == 0)
    sibling = (2 * i + (1 - c), j)

    def forward(k, count, core):
        isrc, jsrc = partner(k, -1)
        x = 3 * isrc + jnp.where(core == 0, 0, 3 - count)
        ref = got.at[pl.ds(x, count), jsrc]
        return ref, pltpu.make_async_remote_copy(
            src_ref=ref,
            dst_ref=ref,
            send_sem=fsend_sem.at[k],
            recv_sem=frecv_sem.at[k],
            device_id=sibling,
            device_id_type=MESH,
        )

    def pass_on(k, carry):
        def one(count):
            ref, copy = forward(k, count, c)

            @pl.when(k > 0)
            def _():
                wait_for(ref, recv_sem.at[k])

            pl.when(k + 16 < 64)(lambda: send_to(k + 16, None))
            copy.start()

        pl.when(two)(lambda: one(2))
        pl.when(jnp.logical_not(two))(lambda: one(1))
        return carry

    def accept(k, carry):
        def one(count):
            forward(k, count, 1 - c)[1].wait_recv()

        pl.when(two)(lambda: one(1))
        pl.when(jnp.logical_not(two))(lambda: one(2))
        return carry

    def finish_forward(k, carry):
        def one(count):
            forward(k, count, c)[1].wait_send()

        pl.when(two)(lambda: one(2))
        pl.when(jnp.logical_not(two))(lambda: one(1))
        return carry

    def far(axis, parity, n):
        return (here[axis] + parity + 2 * n) % 4

    def stack_x(x, half):
        for n in range(2):
            js = pl.ds(2 * far(2, half, n), 2)
            tails = jnp.concatenate([got[x, js, 4 + k].reshape(32, 128) for k in range(3)], axis=0)
            tails = jnp.dot(xt_ref[...], tails, preferred_element_type=jnp.float32)
            tails = (tails[:64, :64] + tails[64:, 64:]).astype(jnp.bfloat16)
            used = lax.broadcasted_iota(jnp.int32, (32, 128), 0) % 16 < 11
            for h in range(2):
                at = slice(64 * h + 32 * n, 64 * h + 32 * n + 32)
                for k in range(4):
                    block = got[x, js, 4 * h + k].reshape(32, 128)
                    if h:
                        block = jnp.where(used, block, jnp.zeros_like(block))
                    zbuf[x, half, at, 128 * k : 128 * k + 128] = block
                zbuf[x, half, at, 512:576] = tails[32 * h : 32 * h + 32]

    def stack_y(jd, half):
        for n in range(2):
            xs = pl.ds(6 * far(0, half, n), 6)
            block = jnp.concatenate(
                [
                    jnp.concatenate(
                        [got[xs, jd, 4 * h + k].reshape(96, 128) for k in range(4)], axis=1
                    )
                    for h in range(2)
                ],
                axis=0,
            )
            rows = jnp.dot(py_ref[...], block, preferred_element_type=jnp.float32)
            tails = jnp.concatenate([got[xs, jd, 4 + k].reshape(96, 128) for k in range(3)], axis=0)
            tails = jnp.dot(yt_ref[...], tails, preferred_element_type=jnp.float32)
            tail = tails[:192, :64] + tails[192:, 64:]
            rows = jnp.concatenate([rows, tail], axis=1).astype(jnp.bfloat16)
            for y in range(3):
                zbuf[3 * jd + y, half, 64 * n : 64 * n + 64] = rows[64 * y : 64 * y + 64]

    def turn(p, half):
        for w in range(2):
            for start, width in ((0, 256), (256, 256), (512, 64)):
                turned[w, start : start + width] = lax.dot_general(
                    eye_ref[:width, :width],
                    zbuf[2 * p + w, half, :, start : start + width],
                    NT,
                    preferred_element_type=jnp.float32,
                )
        rows_at = pl.ds(pl.multiple_of(48 * p, 16), 48)
        for z in range(24):
            cols = slice(128 * z, 128 * z + 128)
            straight = [turned[w, 24 * z : 24 * z + 24] for w in range(2)]
            m_ref[0, half, rows_at, cols] = jnp.concatenate(straight, 0).astype(jnp.bfloat16)
            strided = [turned[w, pl.ds(z, 24, stride=24)] for w in range(2)]
            m_ref[1, half, rows_at, cols] = jnp.concatenate(strided, 0).astype(jnp.bfloat16)

    scale = 1.0 / CHI**3

    def moved(axis, to):
        to_coords = [to if a == axis else here[a] for a in range(3)]
        di, dj = chip_at(*to_coords)
        return 2 * di + c, dj

    def axes(part):
        return part, (part + 1) % 3, (part + 2) % 3

    def stage1(which):
        for part in range(3):
            first = axes(part)[0]
            at = here[first]

            def rows(to, e, part=part):
                n = jnp.where(c == which, unit_of(part, 0, to, e), unit_of(part, 1, to, e))
                return pl.ds(pl.multiple_of(CHI * n, 8), CHI)

            def send(step, carry, part=part, first=first, at=at, rows=rows):
                to = (at + step) % 4
                for e in range(2):
                    pltpu.make_async_remote_copy(
                        src_ref=q_ref.at[which, rows(to, e)],
                        dst_ref=parts1.at[part, which, at, e],
                        send_sem=s1_sem.at[part, which],
                        recv_sem=r1_sem.at[part, which],
                        device_id=moved(first, to),
                        device_id_type=MESH,
                    ).start()
                return carry

            lax.fori_loop(1, 4, send, 0)
            for e in range(2):
                parts1[part, which, at, e] = q_ref[which, rows(at, e)]

    def passing(start, stop):
        lax.fori_loop(jnp.minimum(start, 64), jnp.minimum(stop, 64), pass_on, 0)

    def prepare(legs, half, ahead):
        def per_place(n, carry):
            at = jnp.where(c == 0, far(0, legs, n), far(2, legs, n))

            @pl.when(c == 0)
            def _():
                def per_leg(m, carry):
                    stack_x(6 * at + m, half)
                    return carry

                lax.fori_loop(0, 6, per_leg, 0)

            @pl.when(c == 1)
            def _():
                def per_leg(m, carry):
                    stack_y(2 * at + m, half)
                    return carry

                lax.fori_loop(0, 2, per_leg, 0)

            def per_pair(m, carry):
                turn(3 * at + m, half)
                return carry

            lax.fori_loop(0, 3, per_pair, 0)
            return carry

        lax.fori_loop(0, 2, per_place, 0)

    def gram(which, half):
        for col, width in ((0, 256), (256, 256), (512, 64)):
            before = q_ref[which, col:, col : col + width]
            total = jnp.where(half == 1, before, jnp.zeros_like(before))
            for ks in (slice(0, 1536), slice(1536, 3072)):
                total += lax.dot_general(
                    m_ref[which, half, col:, ks], m_ref[which, half, col : col + width, ks],
                    NT, preferred_element_type=jnp.float32,
                )
            q_ref[which, col:, col : col + width] = total

    def mirror(which):
        for col, width in ((0, 256), (256, 256)):
            below = q_ref[which, col + width :, col : col + width]
            q_ref[which, col : col + width, col + width :] = below.T

    passing(0, 16)

    def quarter(n, carry):
        ahead = 16 * n + 16
        lax.fori_loop(16 * n, ahead, accept, 0)
        near, distant = n % 2, n // 2
        legs = jnp.where(c == 0, distant, near)
        half = jnp.where(c == 0, near, distant)
        prepare(legs, half, ahead)
        last = n == 3
        multiplies = jnp.logical_or(last, n == 2 - c)

        @pl.when(multiplies)
        def _():
            def one(which, carry):
                gram(which, half)

                @pl.when(last)
                def _():
                    mirror(which)
                    stage1(which)

                return carry

            lax.fori_loop(0, 2, one, 0)

        passing(ahead, ahead + 16)
        return carry

    lax.fori_loop(0, 4, quarter, 0)

    def stage2(which):
        for part in range(3):
            first, second, _ = axes(part)
            g, at = here[first], here[second]
            ref = parts1.at[part, which]
            take(ref, 3, r1_sem.at[part, which])
            sums1[part, which] = (ref[0] + ref[1]) + (ref[2] + ref[3])
            for e in range(2):
                to = jnp.where(
                    c == which, second_place(part, 0, g, e), second_place(part, 1, g, e)
                )

                @pl.when(to != at)
                def _(part=part, second=second, at=at, to=to, e=e):
                    pltpu.make_async_remote_copy(
                        src_ref=sums1.at[part, which, e],
                        dst_ref=parts2.at[part, at],
                        send_sem=s2_sem.at[part],
                        recv_sem=r2_sem.at[part],
                        device_id=moved(second, to),
                        device_id_type=MESH,
                    ).start()

                @pl.when(to == at)
                def _(part=part, at=at, e=e):
                    parts2[part, at] = sums1[part, which, e]

    lax.fori_loop(0, 64, finish_forward, 0)

    def drain(u, carry):
        idest = (12 * c + u) % 8
        pl.when(idest == i)(lambda: take(snd.at[u], 7, send_sem.at[u]))
        pl.when(idest != i)(lambda: take(snd.at[u], 8, send_sem.at[u]))
        return carry

    lax.fori_loop(0, 12, drain, 0)

    def both(which, carry):
        stage2(which)
        return carry

    lax.fori_loop(0, 2, both, 0)

    owner = []
    for part in range(3):
        first, second, third = axes(part)
        kind, to = owned_unit(part, here[first], here[second])
        at = here[third]
        owner.append((kind, to == at))
        take(parts2.at[part], 3, r2_sem.at[part])
        total = (parts2[part, 0] + parts2[part, 1]) + (parts2[part, 2] + parts2[part, 3])

        @pl.when(to == at)
        def _(part=part, at=at, total=total):
            parts3[part, at] = total

        @pl.when(to != at)
        def _(part=part, third=third, at=at, to=to, total=total):
            sums2[part] = total
            pltpu.make_async_remote_copy(
                src_ref=sums2.at[part],
                dst_ref=parts3.at[part, at],
                send_sem=s3_sem.at[part],
                recv_sem=r3_sem.at[part],
                device_id=moved(third, to),
                device_id_type=MESH,
            ).start()

    def own_part(part, carry):
        def pick(values):
            return jnp.where(part == 0, values[0], jnp.where(part == 1, values[1], values[2]))

        kind = pick([jnp.where(k, 1, 0) for k, _ in owner]) == 1
        owns = pick([jnp.where(o, 1, 0) for _, o in owner]) == 1
        which = jnp.where(kind, 1 - c, c)

        @pl.when(owns)
        def _():
            take(parts3.at[part], 3, r3_sem.at[part])
            total = (parts3[part, 0] + parts3[part, 1]) + (parts3[part, 2] + parts3[part, 3])
            mine[part] = relayout(total * scale, st_ref, mask_ref)

            def give(step, carry):
                di = jnp.where(kind, (i + step) % 8, i)
                dj = jnp.where(kind, j, (j + step) % 8)
                pltpu.make_async_remote_copy(
                    src_ref=mine.at[part],
                    dst_ref=rows_ab.at[which, part],
                    send_sem=out_sem.at[part],
                    recv_sem=rows_sem.at[which, part],
                    device_id=(2 * di + c, dj),
                    device_id_type=MESH,
                ).start()
                return carry

            lax.fori_loop(1, 8, give, 0)
            rows_ab[which, part] = mine[part]

        return carry

    lax.fori_loop(0, 3, own_part, 0)

    for part in range(3):
        kind, owns = owner[part]
        for which in range(2):
            own = jnp.logical_and(owns, kind == (c != which))

            @pl.when(jnp.logical_not(own))
            def _(part=part, which=which):
                wait_for(rows_ab.at[which, part], rows_sem.at[which, part])

    product = lax.dot_general(
        rows_ab[0].reshape(72, PAIR), rows_ab[1].reshape(72, PAIR), NT,
        precision=HIGHEST, preferred_element_type=jnp.float32,
    ) * scale
    for a in range(3):
        piece[a] = product[CHI * a : CHI * a + CHI]

    def spread_x(first_two):
        for core in range(2):
            count = 2 if first_two == (core == 0) else 1
            start = 0 if core == 0 else 3 - count
            slot = 2 * j + (0 if core == 0 else 2 - count)
            source = piece.at[pl.ds(start, count)]
            target = ox_ref.at[pl.ds(slot, count)]

            def one(step, carry, core=core, source=source, target=target):
                pltpu.make_async_remote_copy(
                    src_ref=source,
                    dst_ref=target,
                    send_sem=x_sem.at[core],
                    recv_sem=rx_sem,
                    device_id=(2 * i + core, (j + step) % 8),
                    device_id_type=MESH,
                ).start()
                return carry

            lax.fori_loop(1 if core == 0 else 0, 8, one, 0)
            if core == 0:
                for a in range(count):
                    ox_ref[slot + a] = piece[start + a]

    swap = pltpu.make_async_remote_copy(
        src_ref=oy_ref,
        dst_ref=oy_ref,
        send_sem=both_sem.at[0],
        recv_sem=both_sem.at[1],
        device_id=(2 * i, j),
        device_id_type=MESH,
    )

    @pl.when(jnp.logical_and(c == 0, j < 4))
    def _():
        spread_x(True)

    @pl.when(jnp.logical_and(c == 0, j >= 4))
    def _():
        spread_x(False)

    @pl.when(c == 1)
    def _():
        def one(step, carry):
            pltpu.make_async_remote_copy(
                src_ref=piece,
                dst_ref=oy_ref.at[i],
                send_sem=y_sem,
                recv_sem=ry_sem,
                device_id=(2 * ((i + step) % 8) + 1, j),
                device_id_type=MESH,
            ).start()
            return carry

        lax.fori_loop(1, 8, one, 0)
        oy_ref[i] = piece[...]
        take(oy_ref, 7, ry_sem)
        swap.start()

    for part in range(3):
        for which in range(2):
            take(parts1.at[part, which], 3, s1_sem.at[part, which])
        take(parts2.at[part], 3, s2_sem.at[part])
        owns = owner[part][1]
        pl.when(jnp.logical_not(owns))(
            lambda part=part: wait_for(sums2.at[part], s3_sem.at[part])
        )
        pl.when(owns)(
            lambda part=part: wait_for(q_ref.at[0, pl.ds(0, 7 * CHI)], out_sem.at[part])
        )


    @pl.when(jnp.logical_and(c == 0, j < 4))
    def _():
        take(ox_ref, 14, x_sem.at[0])
        take(ox_ref, 8, x_sem.at[1])
        take(ox_ref, 10, rx_sem)

    @pl.when(jnp.logical_and(c == 0, j >= 4))
    def _():
        take(ox_ref, 7, x_sem.at[0])
        take(ox_ref, 16, x_sem.at[1])
        take(ox_ref, 11, rx_sem)

    @pl.when(c == 0)
    def _():
        swap.wait_recv()

    @pl.when(c == 1)
    def _():
        take(ox_ref, 12, rx_sem)
        take(oy_ref, 7, y_sem)
        swap.wait_send()


def per_device(tensor, trial_x, trial_y):
    vmem = pl.BlockSpec(memory_space=pltpu.VMEM)
    dma = pltpu.SemaphoreType.DMA
    index = np.arange(PAIR)
    tile = (np.arange(72)[:, None] % CHI == index[None, :] % CHI).astype(np.float32)
    mask = (np.arange(CHI)[:, None] == index[None, :] // CHI).astype(np.float32)
    f32, bf16 = jnp.float32, jnp.bfloat16
    out_x, out_y = pl.pallas_call(
        fused_kernel,
        out_shape=[
            jax.ShapeDtypeStruct((16, CHI, 72), f32),
            jax.ShapeDtypeStruct((8, 3, CHI, 72), f32),
        ],
        in_specs=[pl.BlockSpec(memory_space=pl.ANY)] + [vmem] * 8,
        out_specs=[vmem] * 2,
        scratch_shapes=[
            pltpu.VMEM((12, 216, PAIR), bf16),
            dma((12,)),
            pltpu.VMEM((12, 8, 8, 16, 128), bf16),
            pltpu.VMEM((24, 8, 8, 16, 128), bf16),
            pltpu.VMEM((24, 2, 128, PAIR), bf16),
            pltpu.VMEM((2, PAIR, 128), f32),
            pltpu.VMEM((2, 2, PAIR, 24 * 128), bf16),
            pltpu.VMEM((2, PAIR, PAIR), f32),
            dma((12,)), dma((64,)), dma((64,)), dma((64,)),
            pltpu.VMEM((3, 2, 4, 2, CHI, PAIR), f32),
            pltpu.VMEM((3, 4, CHI, PAIR), f32),
            pltpu.VMEM((3, 4, CHI, PAIR), f32),
            pltpu.VMEM((3, 2, 2, CHI, PAIR), f32),
            pltpu.VMEM((3, CHI, PAIR), f32),
            pltpu.VMEM((3, CHI, PAIR), f32),
            pltpu.VMEM((2, 3, CHI, PAIR), f32),
            pltpu.VMEM((3, CHI, 72), f32),
            dma((3, 2)), dma((3, 2)), dma((3,)), dma((3,)), dma((3,)), dma((3,)),
            dma((3,)), dma((2, 3)), dma((2,)), dma, dma, dma, dma((2,)),
        ],
        compiler_params=pltpu.CompilerParams(
            collective_id=0, has_side_effects=True, vmem_limit_bytes=62 * 2**20
        ),
        name="hotrg_step",
    )(
        tensor.reshape(12, 216, PAIR),
        jnp.asarray(send_rows(), bf16),
        jnp.asarray(send_tails(), bf16),
        jnp.asarray(y_rows(), bf16),
        jnp.asarray(x_tails(), bf16),
        jnp.asarray(y_tails(), bf16),
        jnp.asarray(np.eye(256), bf16),
        jnp.asarray(tile, bf16),
        jnp.asarray(mask, f32),
    )

    core = lax.axis_index("aa") % 2
    rows_x = out_x.reshape(8, 2, CHI, 3, CHI).transpose(1, 0, 3, 2, 4).reshape(48, PAIR)
    gram_x = lax.dynamic_slice_in_dim(rows_x, core * 12, 36, 0)
    gram_y = out_y.reshape(8, 3, CHI, 3, CHI).transpose(1, 0, 3, 2, 4).reshape(72, PAIR)
    proj_x = jnp.dot(gram_x, trial_x, precision=HIGHEST, preferred_element_type=jnp.float32)
    proj_y = jnp.dot(gram_y, trial_y, precision=HIGHEST, preferred_element_type=jnp.float32)
    return (gram_x, proj_x, gram_y, proj_y)


def solution(mesh):
    in_specs = (P("aa", "ba", None), P(), P())
    out_specs = (P("aa", None), P("aa", None), P("ba", None), P("ba", None))
    return jax.shard_map(
        per_device, mesh=mesh, in_specs=in_specs, out_specs=out_specs, check_vma=False
    )
```

```python
import functools

import jax
import jax.numpy as jnp
import numpy as np
from jax import lax
from jax.experimental import pallas as pl
from jax.experimental.pallas import tpu as pltpu
from jax.sharding import PartitionSpec as P

CHI = 24
PAIR = 576
GROUPS = 8
MSG = 32
STACK = GROUPS * MSG
HIGHEST = lax.Precision.HIGHEST
MESH = pl.DeviceIdType.MESH
NT = (((1,), (1,)), ((), ()))


def send_rows():
    out = np.zeros((STACK, 216), np.float32)
    for jd in range(8):
        for xs in range(3):
            for y in range(3):
                for ys in range(3):
                    h, r = divmod(xs * 9 + y * 3 + ys, 16)
                    out[h * 128 + jd * 16 + r, xs * 72 + y * 24 + jd * 3 + ys] = 1
    return out


def tail_slot(r):
    return (r % 14) // 5, 11 + (r % 14) % 5


def send_tails():
    out = np.zeros((2, 3, 8, 16, 216), np.float32)
    for jd in range(8):
        for xs in range(3):
            for y in range(3):
                for ys in range(3):
                    r = xs * 9 + y * 3 + ys
                    k, row = tail_slot(r)
                    out[r // 14, k, jd, row, xs * 72 + y * 24 + jd * 3 + ys] = 1
    return out.reshape(768, 216)


def x_tails():
    out = np.zeros((2, 2, 2, 16, 3, 2, 16), np.float32)
    for jj in range(2):
        for r in range(27):
            k, row = tail_slot(r)
            out[r // 14, r // 16, jj, r % 16, k, jj, row] = 1
    return out.reshape(128, 96)


def y_tails():
    out = np.zeros((2, 192, 3, 6, 16), np.float32)
    for xg in range(6):
        for xs in range(3):
            for y in range(3):
                for ys in range(3):
                    r = xs * 9 + y * 3 + ys
                    k, row = tail_slot(r)
                    out[r // 14, y * 64 + xg * 9 + xs * 3 + ys, k, xg, row] = 1
    return out.reshape(384, 288)


def y_rows():
    out = np.zeros((192, 192), np.float32)
    for xg in range(6):
        for xs in range(3):
            for y in range(3):
                for ys in range(3):
                    h, r = divmod(xs * 9 + y * 3 + ys, 16)
                    out[y * 64 + xg * 9 + xs * 3 + ys, h * 96 + xg * 16 + r] = 1
    return out


def place():
    aa = lax.axis_index("aa")
    ba = lax.axis_index("ba")
    return aa // 2, aa % 2, ba


def coordinates():
    aa = lax.axis_index("aa")
    ba = lax.axis_index("ba")
    return aa // 4, (aa // 2) % 2 + 2 * (ba % 2), ba // 2


def chip_at(z, x, y):
    return 2 * z + x % 2, 2 * y + x // 2


def shift_of(k):
    quarter, rest = k // 16, k % 16
    low, high = rest % 4, rest // 4
    dz = 2 * (low % 2) + quarter // 2
    dx = (low + high) % 4
    dy = 2 * ((high + low // 2) % 2) + quarter % 2
    return dz, dx, dy


def partner(k, sign):
    z, x, y = coordinates()
    dz, dx, dy = shift_of(k)
    return chip_at((z + 4 + sign * dz) % 4, (x + 4 + sign * dx) % 4, (y + 4 + sign * dy) % 4)


def wait_for(ref, sem):
    pltpu.make_async_copy(ref, ref, sem).wait()


def take(ref, count, sem):
    wait_for(ref.at[pl.ds(0, count)], sem)


def greet(i, c, j, barrier):
    def one(n, carry):
        di, dj = n // 8, n % 8

        @pl.when(jnp.logical_not(jnp.logical_and(di == i, dj == j)))
        def _():
            pl.semaphore_signal(barrier, inc=1, device_id=(2 * di + c, dj), device_id_type=MESH)

        return carry

    lax.fori_loop(0, 64, one, 0)

    @pl.when(c == 0)
    def _():
        pl.semaphore_signal(barrier, inc=1, device_id=(2 * i + 1, j), device_id_type=MESH)

    @pl.when(c == 1)
    def _():
        def across(n, carry):
            pl.semaphore_signal(barrier, inc=1, device_id=(2 * i, n), device_id_type=MESH)
            return carry

        lax.fori_loop(0, 8, across, 0)


def relayout(block, st_ref, mask_ref):
    high = block.astype(jnp.bfloat16).astype(jnp.float32)
    mid = (block - high).astype(jnp.bfloat16).astype(jnp.float32)
    terms = (high, mid, block - high - mid)
    spread = jnp.concatenate(
        [
            jnp.concatenate([term[:, CHI * q : CHI * q + CHI] for term in terms], axis=1)
            for q in range(CHI)
        ],
        axis=0,
    )
    tiled = jnp.dot(spread.astype(jnp.bfloat16), st_ref[...], preferred_element_type=jnp.float32)
    return jnp.sum(tiled.reshape(CHI, CHI, PAIR) * mask_ref[...][None, :, :], axis=1)


def unit_of(part, kind, g, e):
    if part == 0:
        hi, lo = g, e
    elif part == 1:
        hi, lo = (2 * (g % 2) + e, g // 2) if kind else (2 * (g // 2) + e, g % 2)
    else:
        hi, lo = (g, e) if kind else (2 * (g // 2) + e, g % 2)
    return 6 * hi + 3 * lo + part


def second_place(part, kind, g, e):
    if part == 0:
        return 1 + e if kind else 3 * e
    half = (g % 2 if kind else 1 - g % 2) if part == 1 else (1 - g // 2 if kind else g // 2)
    return 2 * half + e


def owned_unit(part, g, m):
    if part == 0:
        kind = (m == 1) | (m == 2)
        return kind, jnp.where(kind, g, (g + 2 * m + 3) % 4)
    if part == 1:
        kind = m // 2 == g % 2
        return kind, jnp.where(kind, (2 * g + 3 * m + 2) % 4, 2 * (g // 2) + m % 2)
    kind = m // 2 != g // 2
    return kind, jnp.where(kind, 2 * (m % 2) + (m + 1) % 2, g % 2 + 2 * (m % 2))


def fused_kernel(
    t_ref, ps_ref, pt_ref, py_ref, xt_ref, yt_ref, eye_ref, st_ref, mask_ref, ox_ref, oy_ref,
    unit, load_sem, snd, got, zbuf, turned, m_ref, q_ref,
    send_sem, recv_sem, fsend_sem, frecv_sem,
    parts1, parts2, parts3, sums1, sums2, mine, rows_ab, piece,
    s1_sem, r1_sem, s2_sem, r2_sem, s3_sem, r3_sem, out_sem, rows_sem, x_sem, rx_sem, y_sem, ry_sem,
    both_sem,
):
    i, c, j = place()
    here = coordinates()
    barrier = pltpu.get_barrier_semaphore()
    greet(i, c, j, barrier)

    def load(u):
        return pltpu.make_async_copy(t_ref.at[u], unit.at[u], load_sem.at[u])

    def start_load(u, carry):
        load(u).start()
        return carry

    lax.fori_loop(0, 12, start_load, 0)

    def gather_unit(u, carry):
        load(u).wait()
        rows = jnp.dot(ps_ref[...], unit[u], preferred_element_type=jnp.float32)
        ends = unit[u, :, 512:]
        ends = jnp.dot(
            pt_ref[...], jnp.concatenate([ends, ends], axis=1), preferred_element_type=jnp.float32
        )
        left = lax.broadcasted_iota(jnp.int32, (128, 128), 1) < 64
        for k in range(4):
            cols = slice(128 * k, 128 * k + 128)
            second = rows[128:, cols]
            if k < 3:
                at = 128 * k
                second += jnp.where(left, ends[at : at + 128], ends[384 + at : 512 + at])
            snd[u, :, k] = rows[:128, cols].astype(jnp.bfloat16).reshape(8, 16, 128)
            snd[u, :, 4 + k] = second.astype(jnp.bfloat16).reshape(8, 16, 128)
        return carry

    lax.fori_loop(0, 12, gather_unit, 0)
    pl.when(c == 0)(lambda: pl.semaphore_wait(barrier, 71))
    pl.when(c == 1)(lambda: pl.semaphore_wait(barrier, 64))

    def send_unit(u, k, idest, jdest):
        x = 3 * i + (12 * c + u) // 8

        @pl.when(k > 0)
        def _():
            pltpu.make_async_remote_copy(
                src_ref=snd.at[u, jdest],
                dst_ref=got.at[x, j],
                send_sem=send_sem.at[u],
                recv_sem=recv_sem.at[k],
                device_id=(2 * idest + c, jdest),
                device_id_type=MESH,
            ).start()

        @pl.when(k == 0)
        def _():
            got[x, j] = snd[u, jdest]

    def send_to(k, carry):
        idest, jdest = partner(k, 1)
        first = (idest + 4 * c) % 8
        send_unit(first, k, idest, jdest)

        @pl.when(first < 4)
        def _():
            send_unit(first + 8, k, idest, jdest)

        return carry

    lax.fori_loop(0, 16, send_to, 0)

    two = (i < 4) == (c == 0)
    sibling = (2 * i + (1 - c), j)

    def forward(k, count, core):
        isrc, jsrc = partner(k, -1)
        x = 3 * isrc + jnp.where(core == 0, 0, 3 - count)
        ref = got.at[pl.ds(x, count), jsrc]
        return ref, pltpu.make_async_remote_copy(
            src_ref=ref,
            dst_ref=ref,
            send_sem=fsend_sem.at[k],
            recv_sem=frecv_sem.at[k],
            device_id=sibling,
            device_id_type=MESH,
        )

    def pass_on(k, carry):
        def one(count):
            ref, copy = forward(k, count, c)

            @pl.when(k > 0)
            def _():
                wait_for(ref, recv_sem.at[k])

            pl.when(k + 16 < 64)(lambda: send_to(k + 16, None))
            copy.start()

        pl.when(two)(lambda: one(2))
        pl.when(jnp.logical_not(two))(lambda: one(1))
        return carry

    def accept(k, carry):
        def one(count):
            forward(k, count, 1 - c)[1].wait_recv()

        pl.when(two)(lambda: one(1))
        pl.when(jnp.logical_not(two))(lambda: one(2))
        return carry

    def finish_forward(k, carry):
        def one(count):
            forward(k, count, c)[1].wait_send()

        pl.when(two)(lambda: one(2))
        pl.when(jnp.logical_not(two))(lambda: one(1))
        return carry

    def far(axis, parity, n):
        return (here[axis] + parity + 2 * n) % 4

    def stack_x(x, half):
        for n in range(2):
            js = pl.ds(2 * far(2, half, n), 2)
            tails = jnp.concatenate([got[x, js, 4 + k].reshape(32, 128) for k in range(3)], axis=0)
            tails = jnp.dot(xt_ref[...], tails, preferred_element_type=jnp.float32)
            tails = (tails[:64, :64] + tails[64:, 64:]).astype(jnp.bfloat16)
            used = lax.broadcasted_iota(jnp.int32, (32, 128), 0) % 16 < 11
            for h in range(2):
                at = slice(64 * h + 32 * n, 64 * h + 32 * n + 32)
                for k in range(4):
                    block = got[x, js, 4 * h + k].reshape(32, 128)
                    if h:
                        block = jnp.where(used, block, jnp.zeros_like(block))
                    zbuf[x, half, at, 128 * k : 128 * k + 128] = block
                zbuf[x, half, at, 512:576] = tails[32 * h : 32 * h + 32]

    def stack_y(jd, half):
        for n in range(2):
            xs = pl.ds(6 * far(0, half, n), 6)
            block = jnp.concatenate(
                [
                    jnp.concatenate(
                        [got[xs, jd, 4 * h + k].reshape(96, 128) for k in range(4)], axis=1
                    )
                    for h in range(2)
                ],
                axis=0,
            )
            rows = jnp.dot(py_ref[...], block, preferred_element_type=jnp.float32)
            tails = jnp.concatenate([got[xs, jd, 4 + k].reshape(96, 128) for k in range(3)], axis=0)
            tails = jnp.dot(yt_ref[...], tails, preferred_element_type=jnp.float32)
            tail = tails[:192, :64] + tails[192:, 64:]
            rows = jnp.concatenate([rows, tail], axis=1).astype(jnp.bfloat16)
            for y in range(3):
                zbuf[3 * jd + y, half, 64 * n : 64 * n + 64] = rows[64 * y : 64 * y + 64]

    def turn(p, half):
        for w in range(2):
            for start, width in ((0, 256), (256, 256), (512, 64)):
                turned[w, start : start + width] = lax.dot_general(
                    eye_ref[:width, :width],
                    zbuf[2 * p + w, half, :, start : start + width],
                    NT,
                    preferred_element_type=jnp.float32,
                )
        rows_at = pl.ds(pl.multiple_of(48 * p, 16), 48)
        for z in range(24):
            cols = slice(128 * z, 128 * z + 128)
            straight = [turned[w, 24 * z : 24 * z + 24] for w in range(2)]
            m_ref[0, half, rows_at, cols] = jnp.concatenate(straight, 0).astype(jnp.bfloat16)
            strided = [turned[w, pl.ds(z, 24, stride=24)] for w in range(2)]
            m_ref[1, half, rows_at, cols] = jnp.concatenate(strided, 0).astype(jnp.bfloat16)

    scale = 1.0 / CHI**3

    def moved(axis, to):
        to_coords = [to if a == axis else here[a] for a in range(3)]
        di, dj = chip_at(*to_coords)
        return 2 * di + c, dj

    def axes(part):
        return part, (part + 1) % 3, (part + 2) % 3

    def stage1(which):
        for part in range(3):
            first = axes(part)[0]
            at = here[first]

            def rows(to, e, part=part):
                n = jnp.where(c == which, unit_of(part, 0, to, e), unit_of(part, 1, to, e))
                return pl.ds(pl.multiple_of(CHI * n, 8), CHI)

            def send(step, carry, part=part, first=first, at=at, rows=rows):
                to = (at + step) % 4
                for e in range(2):
                    pltpu.make_async_remote_copy(
                        src_ref=q_ref.at[which, rows(to, e)],
                        dst_ref=parts1.at[part, which, at, e],
                        send_sem=s1_sem.at[part, which],
                        recv_sem=r1_sem.at[part, which],
                        device_id=moved(first, to),
                        device_id_type=MESH,
                    ).start()
                return carry

            lax.fori_loop(1, 4, send, 0)
            for e in range(2):
                parts1[part, which, at, e] = q_ref[which, rows(at, e)]

    def passing(start, stop):
        lax.fori_loop(jnp.minimum(start, 64), jnp.minimum(stop, 64), pass_on, 0)

    def prepare(legs, half, ahead):
        def per_place(n, carry):
            at = jnp.where(c == 0, far(0, legs, n), far(2, legs, n))

            @pl.when(c == 0)
            def _():
                def per_leg(m, carry):
                    stack_x(6 * at + m, half)
                    return carry

                lax.fori_loop(0, 6, per_leg, 0)

            @pl.when(c == 1)
            def _():
                def per_leg(m, carry):
                    stack_y(2 * at + m, half)
                    return carry

                lax.fori_loop(0, 2, per_leg, 0)

            def per_pair(m, carry):
                turn(3 * at + m, half)
                return carry

            lax.fori_loop(0, 3, per_pair, 0)
            return carry

        lax.fori_loop(0, 2, per_place, 0)

    def gram(which, half):
        for col, width in ((0, 256), (256, 256), (512, 64)):
            before = q_ref[which, col:, col : col + width]
            total = jnp.where(half == 1, before, jnp.zeros_like(before))
            for ks in (slice(0, 3072),):
                total += lax.dot_general(
                    m_ref[which, half, col:, ks], m_ref[which, half, col : col + width, ks],
                    NT, preferred_element_type=jnp.float32,
                )
            q_ref[which, col:, col : col + width] = total

    def mirror(which):
        for col, width in ((0, 256), (256, 256)):
            below = q_ref[which, col + width :, col : col + width]
            q_ref[which, col : col + width, col + width :] = below.T

    passing(0, 16)

    def quarter(n, carry):
        ahead = 16 * n + 16
        lax.fori_loop(16 * n, ahead, accept, 0)
        near, distant = n % 2, n // 2
        legs = jnp.where(c == 0, distant, near)
        half = jnp.where(c == 0, near, distant)
        prepare(legs, half, ahead)
        last = n == 3
        multiplies = jnp.logical_or(last, n == 2 - c)

        @pl.when(multiplies)
        def _():
            def one(which, carry):
                gram(which, half)

                @pl.when(last)
                def _():
                    mirror(which)
                    stage1(which)

                return carry

            lax.fori_loop(0, 2, one, 0)

        passing(ahead, ahead + 16)
        return carry

    lax.fori_loop(0, 4, quarter, 0)

    def stage2(which):
        for part in range(3):
            first, second, _ = axes(part)
            g, at = here[first], here[second]
            ref = parts1.at[part, which]
            take(ref, 3, r1_sem.at[part, which])
            sums1[part, which] = (ref[0] + ref[1]) + (ref[2] + ref[3])
            for e in range(2):
                to = jnp.where(
                    c == which, second_place(part, 0, g, e), second_place(part, 1, g, e)
                )

                @pl.when(to != at)
                def _(part=part, second=second, at=at, to=to, e=e):
                    pltpu.make_async_remote_copy(
                        src_ref=sums1.at[part, which, e],
                        dst_ref=parts2.at[part, at],
                        send_sem=s2_sem.at[part],
                        recv_sem=r2_sem.at[part],
                        device_id=moved(second, to),
                        device_id_type=MESH,
                    ).start()

                @pl.when(to == at)
                def _(part=part, at=at, e=e):
                    parts2[part, at] = sums1[part, which, e]

    lax.fori_loop(0, 64, finish_forward, 0)

    def drain(u, carry):
        idest = (12 * c + u) % 8
        pl.when(idest == i)(lambda: take(snd.at[u], 7, send_sem.at[u]))
        pl.when(idest != i)(lambda: take(snd.at[u], 8, send_sem.at[u]))
        return carry

    lax.fori_loop(0, 12, drain, 0)

    def both(which, carry):
        stage2(which)
        return carry

    lax.fori_loop(0, 2, both, 0)

    owner = []
    for part in range(3):
        first, second, third = axes(part)
        kind, to = owned_unit(part, here[first], here[second])
        at = here[third]
        owner.append((kind, to == at))
        take(parts2.at[part], 3, r2_sem.at[part])
        total = (parts2[part, 0] + parts2[part, 1]) + (parts2[part, 2] + parts2[part, 3])

        @pl.when(to == at)
        def _(part=part, at=at, total=total):
            parts3[part, at] = total

        @pl.when(to != at)
        def _(part=part, third=third, at=at, to=to, total=total):
            sums2[part] = total
            pltpu.make_async_remote_copy(
                src_ref=sums2.at[part],
                dst_ref=parts3.at[part, at],
                send_sem=s3_sem.at[part],
                recv_sem=r3_sem.at[part],
                device_id=moved(third, to),
                device_id_type=MESH,
            ).start()

    def own_part(part, carry):
        def pick(values):
            return jnp.where(part == 0, values[0], jnp.where(part == 1, values[1], values[2]))

        kind = pick([jnp.where(k, 1, 0) for k, _ in owner]) == 1
        owns = pick([jnp.where(o, 1, 0) for _, o in owner]) == 1
        which = jnp.where(kind, 1 - c, c)

        @pl.when(owns)
        def _():
            take(parts3.at[part], 3, r3_sem.at[part])
            total = (parts3[part, 0] + parts3[part, 1]) + (parts3[part, 2] + parts3[part, 3])
            mine[part] = relayout(total * scale, st_ref, mask_ref)

            def give(step, carry):
                di = jnp.where(kind, (i + step) % 8, i)
                dj = jnp.where(kind, j, (j + step) % 8)
                pltpu.make_async_remote_copy(
                    src_ref=mine.at[part],
                    dst_ref=rows_ab.at[which, part],
                    send_sem=out_sem.at[part],
                    recv_sem=rows_sem.at[which, part],
                    device_id=(2 * di + c, dj),
                    device_id_type=MESH,
                ).start()
                return carry

            lax.fori_loop(1, 8, give, 0)
            rows_ab[which, part] = mine[part]

        return carry

    lax.fori_loop(0, 3, own_part, 0)

    for part in range(3):
        kind, owns = owner[part]
        for which in range(2):
            own = jnp.logical_and(owns, kind == (c != which))

            @pl.when(jnp.logical_not(own))
            def _(part=part, which=which):
                wait_for(rows_ab.at[which, part], rows_sem.at[which, part])

    product = lax.dot_general(
        rows_ab[0].reshape(72, PAIR), rows_ab[1].reshape(72, PAIR), NT,
        precision=HIGHEST, preferred_element_type=jnp.float32,
    ) * scale
    for a in range(3):
        piece[a] = product[CHI * a : CHI * a + CHI]

    def spread_x(first_two):
        for core in range(2):
            count = 2 if first_two == (core == 0) else 1
            start = 0 if core == 0 else 3 - count
            slot = 2 * j + (0 if core == 0 else 2 - count)
            source = piece.at[pl.ds(start, count)]
            target = ox_ref.at[pl.ds(slot, count)]

            def one(step, carry, core=core, source=source, target=target):
                pltpu.make_async_remote_copy(
                    src_ref=source,
                    dst_ref=target,
                    send_sem=x_sem.at[core],
                    recv_sem=rx_sem,
                    device_id=(2 * i + core, (j + step) % 8),
                    device_id_type=MESH,
                ).start()
                return carry

            lax.fori_loop(1 if core == 0 else 0, 8, one, 0)
            if core == 0:
                for a in range(count):
                    ox_ref[slot + a] = piece[start + a]

    swap = pltpu.make_async_remote_copy(
        src_ref=oy_ref,
        dst_ref=oy_ref,
        send_sem=both_sem.at[0],
        recv_sem=both_sem.at[1],
        device_id=(2 * i, j),
        device_id_type=MESH,
    )

    @pl.when(jnp.logical_and(c == 0, j < 4))
    def _():
        spread_x(True)

    @pl.when(jnp.logical_and(c == 0, j >= 4))
    def _():
        spread_x(False)

    @pl.when(c == 1)
    def _():
        def one(step, carry):
            pltpu.make_async_remote_copy(
                src_ref=piece,
                dst_ref=oy_ref.at[i],
                send_sem=y_sem,
                recv_sem=ry_sem,
                device_id=(2 * ((i + step) % 8) + 1, j),
                device_id_type=MESH,
            ).start()
            return carry

        lax.fori_loop(1, 8, one, 0)
        oy_ref[i] = piece[...]
        take(oy_ref, 7, ry_sem)
        swap.start()

    for part in range(3):
        for which in range(2):
            take(parts1.at[part, which], 3, s1_sem.at[part, which])
        take(parts2.at[part], 3, s2_sem.at[part])
        owns = owner[part][1]
        pl.when(jnp.logical_not(owns))(
            lambda part=part: wait_for(sums2.at[part], s3_sem.at[part])
        )
        pl.when(owns)(
            lambda part=part: wait_for(q_ref.at[0, pl.ds(0, 7 * CHI)], out_sem.at[part])
        )


    @pl.when(jnp.logical_and(c == 0, j < 4))
    def _():
        take(ox_ref, 14, x_sem.at[0])
        take(ox_ref, 8, x_sem.at[1])
        take(ox_ref, 10, rx_sem)

    @pl.when(jnp.logical_and(c == 0, j >= 4))
    def _():
        take(ox_ref, 7, x_sem.at[0])
        take(ox_ref, 16, x_sem.at[1])
        take(ox_ref, 11, rx_sem)

    @pl.when(c == 0)
    def _():
        swap.wait_recv()

    @pl.when(c == 1)
    def _():
        take(ox_ref, 12, rx_sem)
        take(oy_ref, 7, y_sem)
        swap.wait_send()


def per_device(tensor, trial_x, trial_y):
    vmem = pl.BlockSpec(memory_space=pltpu.VMEM)
    dma = pltpu.SemaphoreType.DMA
    index = np.arange(PAIR)
    tile = (np.arange(72)[:, None] % CHI == index[None, :] % CHI).astype(np.float32)
    mask = (np.arange(CHI)[:, None] == index[None, :] // CHI).astype(np.float32)
    f32, bf16 = jnp.float32, jnp.bfloat16
    out_x, out_y = pl.pallas_call(
        fused_kernel,
        out_shape=[
            jax.ShapeDtypeStruct((16, CHI, 72), f32),
            jax.ShapeDtypeStruct((8, 3, CHI, 72), f32),
        ],
        in_specs=[pl.BlockSpec(memory_space=pl.ANY)] + [vmem] * 8,
        out_specs=[vmem] * 2,
        scratch_shapes=[
            pltpu.VMEM((12, 216, PAIR), bf16),
            dma((12,)),
            pltpu.VMEM((12, 8, 8, 16, 128), bf16),
            pltpu.VMEM((24, 8, 8, 16, 128), bf16),
            pltpu.VMEM((24, 2, 128, PAIR), bf16),
            pltpu.VMEM((2, PAIR, 128), f32),
            pltpu.VMEM((2, 2, PAIR, 24 * 128), bf16),
            pltpu.VMEM((2, PAIR, PAIR), f32),
            dma((12,)), dma((64,)), dma((64,)), dma((64,)),
            pltpu.VMEM((3, 2, 4, 2, CHI, PAIR), f32),
            pltpu.VMEM((3, 4, CHI, PAIR), f32),
            pltpu.VMEM((3, 4, CHI, PAIR), f32),
            pltpu.VMEM((3, 2, 2, CHI, PAIR), f32),
            pltpu.VMEM((3, CHI, PAIR), f32),
            pltpu.VMEM((3, CHI, PAIR), f32),
            pltpu.VMEM((2, 3, CHI, PAIR), f32),
            pltpu.VMEM((3, CHI, 72), f32),
            dma((3, 2)), dma((3, 2)), dma((3,)), dma((3,)), dma((3,)), dma((3,)),
            dma((3,)), dma((2, 3)), dma((2,)), dma, dma, dma, dma((2,)),
        ],
        compiler_params=pltpu.CompilerParams(
            collective_id=0, has_side_effects=True, vmem_limit_bytes=62 * 2**20
        ),
        name="hotrg_step",
    )(
        tensor.reshape(12, 216, PAIR),
        jnp.asarray(send_rows(), bf16),
        jnp.asarray(send_tails(), bf16),
        jnp.asarray(y_rows(), bf16),
        jnp.asarray(x_tails(), bf16),
        jnp.asarray(y_tails(), bf16),
        jnp.asarray(np.eye(256), bf16),
        jnp.asarray(tile, bf16),
        jnp.asarray(mask, f32),
    )

    core = lax.axis_index("aa") % 2
    rows_x = out_x.reshape(8, 2, CHI, 3, CHI).transpose(1, 0, 3, 2, 4).reshape(48, PAIR)
    gram_x = lax.dynamic_slice_in_dim(rows_x, core * 12, 36, 0)
    gram_y = out_y.reshape(8, 3, CHI, 3, CHI).transpose(1, 0, 3, 2, 4).reshape(72, PAIR)
    proj_x = jnp.dot(gram_x, trial_x, precision=HIGHEST, preferred_element_type=jnp.float32)
    proj_y = jnp.dot(gram_y, trial_y, precision=HIGHEST, preferred_element_type=jnp.float32)
    return (gram_x, proj_x, gram_y, proj_y)


def solution(mesh):
    in_specs = (P("aa", "ba", None), P(), P())
    out_specs = (P("aa", None), P("aa", None), P("ba", None), P("ba", None))
    return jax.shard_map(
        per_device, mesh=mesh, in_specs=in_specs, out_specs=out_specs, check_vma=False
    )
```
